256 devices in a mesh: tile: 64 (over x, z, core), mem: 4 (over y).
Axes of the slice: x: 4, y: 4, z: 8, core: 2. Of those that a mesh axis runs over, the one named last changes fastest.
Arguments:
- ensemble: bfloat16 [909312, 512], P('tile', 'mem'), may hold values from -6 to 6
- obs_anom: bfloat16 [1024, 64, 512], P('tile', None, 'mem'), may hold values from -6 to 6
- inverses: bfloat16 [1024, 512, 512], P('tile', None, 'mem'), may hold values from -0.02 to 0.1
- innovations: bfloat16 [1024, 64, 512], P('tile', None, 'mem'), may hold values from -6 to 6
- precision: float32 [1024, 64], P('tile'), may hold values from 0.2 to 2
- obs_count: int32 [1024], P('tile'), may hold values from 16 to 64
- loc_tiles: int32 [1024, 4], P('tile'), may hold values from 0 to 63, all different within a row; in each aligned block of 16 rows (0 to 15, 16 to 31, ...) at most 2 rows name the same one
- taper_weight: float32 [1024, 4], P('tile'), may hold values from 0.25 to 1
Outputs:
- analysis: bfloat16 [909312, 512], P('tile', 'mem')
The draws below stay inside these ranges and needn't reach their ends.
Inputs may be any that keep to these rules, and one draw needn't show every extreme that they name: `loc_tiles`: each block names 4 different tiles; among the 16 blocks of one tile's set, no tile is named more than 2 times, a bound that some block reaches.
All inputs are finite; a program needn't handle non-finite values.
Results may differ from the reference program's by a relative error of at most 0.024.
Values may be sent and summed in bfloat16 or wider, within the bound.
No kernel may reach another device: no remote copies, remote signals or barrier semaphores. Data moves between devices by JAX's collectives and lax.ppermute only.
A program may use at most 128 MiB of HBM per device.

```python
import math
import jax
import jax.numpy as jnp
import numpy as np
from jax import lax

K = 512
OB = 64
BLK_DEV = 16
LOC = 4
KM = 128
ROWS_DEV = 14208
ROWS = 909312
NBLK = 1024
CAP = 2
N_TILE = 64
N_MEM = 4


def draw_inverses(key, part):
    key = jax.random.fold_in(key, 11)
    diag_key, noise_key = jax.random.split(key)
    diag_vals = jax.random.uniform(diag_key, (NBLK, K, 1), jnp.float32, 1.0, 2.0)
    noise = jax.random.truncated_normal(noise_key, -4.0, 4.0, (NBLK, K, K), jnp.float32)
    row_ids = lax.broadcasted_iota(jnp.int32, (1, K, K), 1)
    col_ids = lax.broadcasted_iota(jnp.int32, (1, K, K), 2)
    identity = (row_ids == col_ids).astype(jnp.float32)
    return (0.03 * (diag_vals * identity + 0.5 / math.sqrt(K) * noise)).astype(jnp.bfloat16)


def touch_ends(values, rng, least, top_value):
    index_at = [jax.random.randint(jax.random.fold_in(rng, axis), (), 0, length) for axis, length in enumerate(values.shape)]
    main_axis = values.shape.index(max(values.shape))
    neighbour = index_at[:main_axis] + [(index_at[main_axis] + 1) % values.shape[main_axis]] + index_at[main_axis + 1:]
    return values.at[tuple(index_at)].set(least).at[tuple(neighbour)].set(top_value)


def steps_of(own_key, extent, cuts, low, largest):
    def one(axis_at, parts):
        draws = jax.random.uniform(jax.random.fold_in(jax.random.fold_in(own_key, 6), axis_at), (parts,), jnp.float32, low / len(cuts), largest / len(cuts))
        return jnp.repeat(jnp.exp(draws), extent[axis_at] // parts).reshape((-1,) + (1,) * (len(extent) - axis_at - 1))

    gain = one(*cuts[0])
    for cut in cuts[1:]:
        gain = gain * one(*cut)
    return gain


def assign_block(key, own, number, rows, count, top, reach, slope):
    sequence = jax.random.permutation(key, count)
    packed, usual = load_shares(count, rows * top, reach, slope, True), load_shares(count, rows * top, reach, slope, False)
    places = jnp.arange(count)

    def named(sizes, rotation):
        used = int((sizes > 0).sum())
        fixed = max(1, used // 4)
        moved = fixed + (places - fixed + rotation * (used - fixed)) % max(1, count - fixed)
        return jnp.zeros((count,), jnp.int32).at[sequence[jnp.where(places < fixed, places, moved)]].set(jnp.asarray(sizes, jnp.int32))

    sizes = jnp.where(number % 4 == 0, named(packed, number // 4), named(usual, number - number // 4 - 1))
    mixed = jax.random.permutation(jax.random.fold_in(own, 3), count)
    giver, taker = mixed[0:count // 2 * 2:2], mixed[1:count // 2 * 2:2]
    margin = jnp.minimum(sizes[giver] - 1, reach - sizes[taker]) // 2
    margin = jnp.where((giver == sequence[0]) | (taker == sequence[0]) | (sizes[taker] == 0), 0, jnp.maximum(margin, 0))
    moved = jax.random.randint(jax.random.fold_in(own, 4), (count // 2,), 0, 1 << 20) % (margin + 1)
    sizes = sizes.at[giver].add(-moved).at[taker].add(moved)
    items = jnp.searchsorted(jnp.cumsum(sizes), jnp.arange(rows * top), side="right").astype(jnp.int32)
    listing = items.reshape(top, rows).T
    listing = listing[jax.random.permutation(jax.random.fold_in(own, 1), rows)]
    rotation = jax.random.randint(jax.random.fold_in(own, 2), (rows, 1), 0, top)
    return jnp.take_along_axis(listing, (jnp.arange(top)[None, :] + rotation) % top, axis=1)


def load_shares(number_of, total, limit, skew, full):
    portions = [(1 << 20) // math.isqrt(rank ** skew) + 1 for rank in range(1, number_of + 1)]
    largest = limit if full else min(limit, max(-(-total // number_of), total * portions[0] // sum(portions)))
    least = 1 if total - largest >= number_of - 1 else 0
    counts, rest = [largest] + [least] * (number_of - 1), total - largest - least * (number_of - 1)
    while rest > 0:
        movable = [i for i in range(1, number_of) if counts[i] < largest] or [i for i in range(1, number_of) if counts[i] < limit]
        pool, budget = sum([portions[i] for i in movable]), rest
        for i in movable:
            addition = min(limit - counts[i], max(1, budget * portions[i] // pool), rest)
            counts[i] = counts[i] + addition
            rest = rest - addition
    return np.array(counts)


def gaussian(stream_key, shape, scale, limit, cuts=(), kind=jnp.bfloat16):
    gain = steps_of(stream_key, shape, cuts, -0.22, 0.18) if cuts else 1.0
    array = jax.random.normal(stream_key, shape, jnp.float32) * scale * gain
    return jnp.minimum(jnp.maximum(array, -limit), limit).astype(kind)


def setup_inputs(seed: int = 0) -> dict:
    seeds = jax.random.split(jax.random.key(seed), 9)
    ensemble = gaussian(seeds[0], (ROWS, K), 1.0, 6.0, ((0, 64), (1, 4)))
    obs_anom = gaussian(seeds[1], (NBLK, OB, K), 1.0, 6.0, ((0, 64), (2, 4)))
    inverses = draw_inverses(jax.random.fold_in(seeds[8], 71), 0)
    innovations = gaussian(seeds[3], (NBLK, OB, K), 1.0, 6.0, ((0, 64), (2, 4)))
    precision = jnp.clip(jnp.exp(math.log(2.0) - 2.3025851 * jax.random.uniform(seeds[4], (NBLK, OB), jnp.float32) ** steps_of(seeds[4], (NBLK, OB), ((0, 64),), -0.2, 0.2)), 0.2, 2.0)
    obs_count = touch_ends(jax.random.randint(seeds[5], (NBLK,), OB // 4, OB + 1), jax.random.fold_in(seeds[5], 1), OB // 4, OB).astype(jnp.int32)
    loc_tiles_keys = jax.random.split(jax.random.fold_in(seeds[6], 1), NBLK // BLK_DEV)
    loc_tiles_turns = jax.random.permutation(jax.random.fold_in(seeds[6], 3), NBLK // BLK_DEV)
    loc_tiles = jax.vmap(lambda own, number: assign_block(jax.random.fold_in(seeds[6], 2), own, number, BLK_DEV, N_TILE, LOC, CAP, 2))(loc_tiles_keys, loc_tiles_turns).reshape((NBLK, LOC))
    taper_weight = jnp.clip(jnp.exp(math.log(1.0) - 1.3862944 * jax.random.uniform(seeds[7], (NBLK, LOC), jnp.float32) ** steps_of(seeds[7], (NBLK, LOC), ((0, 64),), -0.2, 0.2)), 0.25, 1.0)
    return {"ensemble": ensemble, "obs_anom": obs_anom, "inverses": inverses, "innovations": innovations, "precision": precision, "obs_count": obs_count, "loc_tiles": loc_tiles, "taper_weight": taper_weight}


def reference(ensemble, obs_anom, inverses, innovations, precision, obs_count, loc_tiles, taper_weight):
    gain_rows = jnp.einsum('boj,bij->boi', obs_anom.astype(jnp.float32), inverses.astype(jnp.float32))
    scaled_gain = (taper_weight[:, :, None, None] * gain_rows[:, None, :, :]).astype(jnp.bfloat16)
    obs_index = lax.broadcasted_iota(jnp.int32, (NBLK, OB), 1)
    live_rows = (obs_index < obs_count[:, None]).astype(jnp.float32)
    weighted = ((precision * live_rows)[:, :, None] * innovations.astype(jnp.float32)).astype(jnp.bfloat16)
    flat_gain = jnp.concatenate([scaled_gain.reshape(NBLK * LOC, OB, K), jnp.zeros((1, OB, K), jnp.bfloat16)], axis=0)
    padded_innov = jnp.concatenate([weighted, jnp.zeros((1, OB, K), jnp.bfloat16)], axis=0)
    flat_loc = loc_tiles.reshape(NBLK * LOC)
    tile_slabs = ensemble.reshape(N_TILE, ROWS_DEV, K)
    anomaly_scale = 1.0 / math.sqrt(K - 1)

    def one_tile(carried):
        tile_index, rows_in = carried
        chosen = jnp.nonzero(flat_loc == tile_index, size=N_TILE * CAP, fill_value=NBLK * LOC)[0].astype(jnp.int32)
        gains = jnp.take(flat_gain, chosen, axis=0).reshape(N_TILE * CAP * OB, K)
        innov_rows = jnp.take(padded_innov, chosen // LOC, axis=0).reshape(N_TILE * CAP * OB, K)
        transform = lax.dot_general(gains, innov_rows, (((0,), (0,)), ((), ())), preferred_element_type=jnp.float32).astype(jnp.bfloat16)
        states = rows_in.astype(jnp.float32)
        row_mean = lax.optimization_barrier(jnp.sum(states, axis=1, keepdims=True)) / K
        anomalies = ((states - row_mean) * anomaly_scale).astype(jnp.bfloat16)
        increment = jnp.zeros((ROWS_DEV, K), jnp.float32)
        for member_group in range(N_MEM):
            group_part = jnp.dot(anomalies[:, member_group * KM:(member_group + 1) * KM], transform[member_group * KM:(member_group + 1) * KM, :], preferred_element_type=jnp.float32)
            increment = increment + lax.optimization_barrier(group_part.astype(jnp.bfloat16)).astype(jnp.float32)
        return (states + increment).astype(jnp.bfloat16)
    tile_order = jnp.arange(N_TILE, dtype=jnp.int32)
    analysis = lax.map(one_tile, (tile_order, tile_slabs))
    return analysis.reshape(ROWS, K)
```

```python
import functools
import math

import jax
import jax.numpy as jnp
from jax import lax
from jax.experimental import pallas as pl
from jax.experimental.pallas import tpu as pltpu
from jax.sharding import PartitionSpec as P

VMEM_LIMIT = 48 * 1024 * 1024
GROUPS = 4


def gain_kernel(q_ref, obs_ref, inv_ref, own_ref, s1_ref, s2_ref, s3_ref, rows_ref):
    quarter = own_ref.shape[1]
    q = q_ref[0]
    for k in range(obs_ref.shape[0]):
        rows_ref[...] = lax.dot_general(
            obs_ref[k], inv_ref[k], (((1,), (1,)), ((), ())), preferred_element_type=jnp.float32
        )
        for d, out_ref in enumerate((own_ref, s1_ref, s2_ref, s3_ref)):
            start = pl.multiple_of(lax.rem(q + d, GROUPS) * quarter, quarter)
            out_ref[k] = rows_ref[pl.ds(start, quarter), :].astype(out_ref.dtype)


def gain_parts(q, obs_anom, inverses):
    nblock, obs_rows, part = obs_anom.shape
    members = inverses.shape[1]
    quarter = obs_rows // GROUPS
    step = 4
    out = pl.BlockSpec((step, quarter, members), lambda i, q: (i, 0, 0))
    shape = (nblock, quarter, members)
    return pl.pallas_call(
        gain_kernel,
        grid_spec=pltpu.PrefetchScalarGridSpec(
            num_scalar_prefetch=1,
            grid=(nblock // step,),
            in_specs=[
                pl.BlockSpec((step, obs_rows, part), lambda i, q: (i, 0, 0)),
                pl.BlockSpec((step, members, part), lambda i, q: (i, 0, 0)),
            ],
            out_specs=[out] * GROUPS,
            scratch_shapes=[pltpu.VMEM((obs_rows, members), jnp.float32)],
        ),
        out_shape=[jax.ShapeDtypeStruct(shape, jnp.float32)]
        + [jax.ShapeDtypeStruct(shape, jnp.bfloat16)] * 3,
        compiler_params=pltpu.CompilerParams(vmem_limit_bytes=VMEM_LIMIT),
    )(q, obs_anom, inverses)


def scatter_slots(loc_ref, count_ref, out_ref, value_of):
    pairs = loc_ref.shape[0]
    tiles = count_ref.shape[0]
    capacity = out_ref.shape[0] // tiles
    out_ref[...] = jnp.zeros(out_ref.shape, out_ref.dtype)

    def clear(t, _):
        count_ref[t] = 0
        return 0

    def put(p, _):
        tile = loc_ref[p]
        rank = count_ref[tile]
        count_ref[tile] = rank + 1
        out_ref[tile * capacity + rank] = value_of(p)
        return 0

    lax.fori_loop(0, tiles, clear, 0)
    lax.fori_loop(0, pairs, put, 0)


def pack_innov_kernel(loc_count, q_ref, loc_ref, own_ref, r1_ref, r2_ref, r3_ref, out_ref, full_ref, count_ref):
    part = own_ref.shape[2]
    q = q_ref[0]
    for d, ref in enumerate((own_ref, r1_ref, r2_ref, r3_ref)):
        start = pl.multiple_of(lax.rem(q - d + GROUPS, GROUPS) * part, part)
        full_ref[:, :, pl.ds(start, part)] = ref[...]
    scatter_slots(loc_ref, count_ref, out_ref, lambda p: full_ref[p // loc_count])


def pack_gain_kernel(loc_count, loc_ref, taper_ref, own_ref, r1_ref, r2_ref, r3_ref, out_ref, full_ref, count_ref):
    full_ref[...] = (
        own_ref[...]
        + r1_ref[...].astype(jnp.float32)
        + r2_ref[...].astype(jnp.float32)
        + r3_ref[...].astype(jnp.float32)
    )
    scatter_slots(
        loc_ref,
        count_ref,
        out_ref,
        lambda p: (taper_ref[p] * full_ref[p // loc_count]).astype(out_ref.dtype),
    )


def pack(kernel, scalars, parts, full_dtype, members, tiles, slots):
    nblock, quarter, _ = parts[0].shape
    return pl.pallas_call(
        kernel,
        in_specs=[pl.BlockSpec(memory_space=pltpu.SMEM)] * len(scalars)
        + [pl.BlockSpec(memory_space=pltpu.VMEM)] * len(parts),
        out_specs=pl.BlockSpec(memory_space=pltpu.VMEM),
        out_shape=jax.ShapeDtypeStruct((slots, quarter, members), jnp.bfloat16),
        scratch_shapes=[
            pltpu.VMEM((nblock, quarter, members), full_dtype),
            pltpu.SMEM((tiles,), jnp.int32),
        ],
        compiler_params=pltpu.CompilerParams(vmem_limit_bytes=VMEM_LIMIT),
    )(*scalars, *parts)


def transform_kernel(q_ref, gain_ref, innov_ref, own_ref, s1_ref, s2_ref, s3_ref, total_ref):
    step = pl.program_id(0)
    part = own_ref.shape[1]

    @pl.when(step == 0)
    def _():
        total_ref[...] = jnp.zeros_like(total_ref)

    total_ref[...] += lax.dot_general(
        gain_ref[...], innov_ref[...], (((0,), (0,)), ((), ())), preferred_element_type=jnp.float32
    )

    @pl.when(step == pl.num_programs(0) - 1)
    def _():
        q = q_ref[0]
        for d, out_ref in enumerate((own_ref, s1_ref, s2_ref, s3_ref)):
            start = pl.multiple_of(lax.rem(q + d, GROUPS) * part, part)
            out_ref[...] = total_ref[:, pl.ds(start, part)].astype(out_ref.dtype)


def transform_parts(q, gain, innov):
    depth, members = gain.shape
    part = members // GROUPS
    step = 512
    out = pl.BlockSpec((members, part), lambda i, q: (0, 0))
    block = pl.BlockSpec((step, members), lambda i, q: (i, 0))
    return pl.pallas_call(
        transform_kernel,
        grid_spec=pltpu.PrefetchScalarGridSpec(
            num_scalar_prefetch=1,
            grid=(depth // step,),
            in_specs=[block, block],
            out_specs=[out] * GROUPS,
            scratch_shapes=[pltpu.VMEM((members, members), jnp.float32)],
        ),
        out_shape=[jax.ShapeDtypeStruct((members, part), jnp.float32)]
        + [jax.ShapeDtypeStruct((members, part), jnp.bfloat16)] * 3,
        compiler_params=pltpu.CompilerParams(vmem_limit_bytes=VMEM_LIMIT),
    )(q, gain, innov)


def update_kernel(
    half, order_ref, t0_ref, t1_ref, t2_ref, t3_ref, own_ref, a_ref, b_ref, oa_ref, ob_ref,
    out_ref, raw_ref, weights_ref, mean_ref, opp_ref,
):
    step = pl.program_id(0)
    part = own_ref.shape[1]
    members = t0_ref.shape[0]

    @pl.when(step == 0)
    def _():
        total = (
            t0_ref[...]
            + t1_ref[...].astype(jnp.float32)
            + t2_ref[...].astype(jnp.float32)
            + t3_ref[...].astype(jnp.float32)
        ).astype(jnp.bfloat16)
        raw_ref[...] = total.reshape(raw_ref.shape)
        mean_ref[...] = jnp.broadcast_to(
            jnp.sum(total.astype(jnp.float32), axis=0, keepdims=True) / members, mean_ref.shape
        )
        for k in range(GROUPS):
            weights_ref[pl.ds(k * part, part), :part] = raw_ref[order_ref[k]]
        weights_ref[:, part:] = jnp.ones((members, part), jnp.bfloat16)

    @pl.when(step < half)
    def _():
        opp_ref[...] = oa_ref[...]

    @pl.when(step >= half)
    def _():
        opp_ref[...] = ob_ref[...]

    own = own_ref[...]
    states = jnp.concatenate([own, a_ref[...], b_ref[...], opp_ref[...]], axis=1)
    both = jnp.dot(states, weights_ref[...], preferred_element_type=jnp.float32)
    increment = (both[:, :part] - both[:, part:] * mean_ref[0:1, :]) * (1.0 / math.sqrt(members - 1))
    out_ref[...] = (own.astype(jnp.float32) + increment).astype(out_ref.dtype)


def update(order, pieces, own, from_a, from_b, opp_a, opp_b):
    rows, part = own.shape
    members = pieces[0].shape[0]
    step = rows // 12
    half = 6
    whole = pl.BlockSpec((members, part), lambda i, o: (0, 0))
    block = pl.BlockSpec((step, part), lambda i, o: (i, 0))
    return pl.pallas_call(
        functools.partial(update_kernel, half),
        grid_spec=pltpu.PrefetchScalarGridSpec(
            num_scalar_prefetch=1,
            grid=(rows // step,),
            in_specs=[whole] * 4
            + [block] * 3
            + [
                pl.BlockSpec((step, part), lambda i, o: (jnp.minimum(i, half - 1), 0)),
                pl.BlockSpec((step, part), lambda i, o: (jnp.maximum(i - half, 0), 0)),
            ],
            out_specs=block,
            scratch_shapes=[
                pltpu.VMEM((GROUPS, part, part), jnp.bfloat16),
                pltpu.VMEM((members, 2 * part), jnp.bfloat16),
                pltpu.VMEM((8, part), jnp.float32),
                pltpu.VMEM((step, part), jnp.bfloat16),
            ],
        ),
        out_shape=jax.ShapeDtypeStruct((rows, part), jnp.bfloat16),
        compiler_params=pltpu.CompilerParams(vmem_limit_bytes=VMEM_LIMIT),
    )(order, *pieces, own, from_a, from_b, opp_a, opp_b)


def shift(x, d):
    return lax.ppermute(x, "mem", [(i, (i + d) % GROUPS) for i in range(GROUPS)])


def swap_a(x):
    return lax.ppermute(x, "mem", [(0, 1), (1, 0), (2, 3), (3, 2)])


def swap_b(x):
    return lax.ppermute(x, "mem", [(0, 3), (3, 0), (1, 2), (2, 1)])


def per_device(
    ensemble, obs_anom, inverses, innovations, precision, obs_count, loc_tiles, taper_weight
):
    tiles = lax.axis_size("tile")
    nblock, obs_rows, part = obs_anom.shape
    members = part * GROUPS
    rows = ensemble.shape[0]
    loc_count = loc_tiles.shape[1]
    quarter = obs_rows // GROUPS
    slots = tiles * 2
    q = lax.axis_index("mem").astype(jnp.int32)
    q1 = q.reshape(1)
    order = jnp.stack([q, q ^ 1, 3 - q, q ^ 2])
    loc = loc_tiles.reshape(nblock * loc_count)
    taper = taper_weight.reshape(nblock * loc_count)

    position = lax.broadcasted_iota(jnp.int32, (nblock, obs_rows), 1)
    live_rows = (position < obs_count[:, None]).astype(jnp.float32)
    weighted = ((precision * live_rows)[:, :, None] * innovations.astype(jnp.float32)).astype(
        jnp.bfloat16
    )

    def quarter_of(d):
        return lax.dynamic_slice_in_dim(weighted, ((q + d) & (GROUPS - 1)) * quarter, quarter, axis=1)

    innov_parts = [quarter_of(0)] + [shift(quarter_of(d), d) for d in (1, 2, 3)]
    g0, g1, g2, g3 = gain_parts(q1, obs_anom, inverses)
    g1, g2, g3 = shift(g1, 1), shift(g2, 2), shift(g3, 3)
    g1, g2, g3, states = lax.optimization_barrier((g1, g2, g3, ensemble))

    from_a, from_b = swap_a(states), swap_b(states)
    opp_a, opp_b = swap_b(from_a[: rows // 2]), swap_a(from_b[rows // 2 :])

    send_innov = pack(
        functools.partial(pack_innov_kernel, loc_count), (q1, loc), innov_parts, jnp.bfloat16,
        members, tiles, slots,
    )
    recv_innov = lax.all_to_all(send_innov, "tile", split_axis=0, concat_axis=0, tiled=True)
    send_gain = pack(
        functools.partial(pack_gain_kernel, loc_count), (loc, taper), [g0, g1, g2, g3],
        jnp.float32, members, tiles, slots,
    )
    recv_gain = lax.all_to_all(send_gain, "tile", split_axis=0, concat_axis=0, tiled=True)
    t0, t1, t2, t3 = transform_parts(
        q1,
        recv_gain.reshape(slots * quarter, members),
        recv_innov.reshape(slots * quarter, members),
    )
    pieces = [t0, shift(t1, 1), shift(t2, 2), shift(t3, 3)]
    return update(order, pieces, ensemble, from_a, from_b, opp_a, opp_b)


def solution(mesh):
    return jax.shard_map(
        per_device,
        mesh=mesh,
        in_specs=(
            P("tile", "mem"),
            P("tile", None, "mem"),
            P("tile", None, "mem"),
            P("tile", None, "mem"),
            P("tile", None),
            P("tile"),
            P("tile", None),
            P("tile", None),
        ),
        out_specs=P("tile", "mem"),
        check_vma=False,
    )
```

```python
import functools
import math

import jax
import jax.numpy as jnp
from jax import lax
from jax.experimental import pallas as pl
from jax.experimental.pallas import tpu as pltpu
from jax.sharding import PartitionSpec as P

VMEM_LIMIT = 48 * 1024 * 1024
GROUPS = 4


def first_kernel(
    q_ref, obs_ref, inv_ref, innov_ref, precision_ref, count_ref,
    g0_ref, g1_ref, g2_ref, g3_ref, w0_ref, w1_ref, w2_ref, w3_ref, rows_ref, live_ref,
):
    quarter = g0_ref.shape[1]
    obs_rows, part = innov_ref.shape[1:]
    blocks = obs_ref.shape[0]
    q = q_ref[0]
    step = pl.program_id(0)
    starts = [pl.multiple_of(lax.rem(q + d, GROUPS) * quarter, quarter) for d in range(GROUPS)]
    position = lax.broadcasted_iota(jnp.int32, (obs_rows, part), 0)
    for k in range(blocks):
        rows_ref[...] = lax.dot_general(
            obs_ref[k], inv_ref[k], (((1,), (1,)), ((), ())), preferred_element_type=jnp.float32
        )
        block = step * blocks + k
        scale = jnp.broadcast_to(precision_ref[pl.ds(block, 1), :], (part, obs_rows)).T
        live_ref[...] = jnp.where(
            position < count_ref[block], scale * innov_ref[k].astype(jnp.float32), 0.0
        )
        for start, g_ref, w_ref in zip(
            starts, (g0_ref, g1_ref, g2_ref, g3_ref), (w0_ref, w1_ref, w2_ref, w3_ref)
        ):
            g_ref[k] = rows_ref[pl.ds(start, quarter), :].astype(g_ref.dtype)
            w_ref[k] = live_ref[pl.ds(start, quarter), :].astype(w_ref.dtype)


def first_parts(q, obs_anom, inverses, innovations, precision, obs_count):
    nblock, obs_rows, part = obs_anom.shape
    members = inverses.shape[1]
    quarter = obs_rows // GROUPS
    step = 4
    g_out = pl.BlockSpec((step, quarter, members), lambda i, q: (i, 0, 0))
    w_out = pl.BlockSpec((step, quarter, part), lambda i, q: (i, 0, 0))
    g_shape = (nblock, quarter, members)
    rows = pl.BlockSpec((step, obs_rows, part), lambda i, q: (i, 0, 0))
    return pl.pallas_call(
        first_kernel,
        grid_spec=pltpu.PrefetchScalarGridSpec(
            num_scalar_prefetch=1,
            grid=(nblock // step,),
            in_specs=[
                rows,
                pl.BlockSpec((step, members, part), lambda i, q: (i, 0, 0)),
                rows,
                pl.BlockSpec((nblock, obs_rows), lambda i, q: (0, 0)),
                pl.BlockSpec(memory_space=pltpu.SMEM),
            ],
            out_specs=[g_out] * GROUPS + [w_out] * GROUPS,
            scratch_shapes=[
                pltpu.VMEM((obs_rows, members), jnp.float32),
                pltpu.VMEM((obs_rows, part), jnp.float32),
            ],
        ),
        out_shape=[jax.ShapeDtypeStruct(g_shape, jnp.float32)]
        + [jax.ShapeDtypeStruct(g_shape, jnp.bfloat16)] * 3
        + [jax.ShapeDtypeStruct((nblock, quarter, part), jnp.bfloat16)] * 4,
        compiler_params=pltpu.CompilerParams(vmem_limit_bytes=VMEM_LIMIT),
    )(q, obs_anom, inverses, innovations, precision, obs_count)


def scatter_slots(loc_ref, count_ref, out_ref, value_of):
    pairs = loc_ref.shape[0]
    tiles = count_ref.shape[0]
    capacity = out_ref.shape[0] // tiles
    out_ref[...] = jnp.zeros(out_ref.shape, out_ref.dtype)

    def clear(t, _):
        count_ref[t] = 0
        return 0

    def put(p, _):
        tile = loc_ref[p]
        rank = count_ref[tile]
        count_ref[tile] = rank + 1
        out_ref[tile * capacity + rank] = value_of(p)
        return 0

    lax.fori_loop(0, tiles, clear, 0)
    lax.fori_loop(0, pairs, put, 0)


def pack_innov_kernel(loc_count, q_ref, loc_ref, own_ref, r1_ref, r2_ref, r3_ref, out_ref, full_ref, count_ref):
    part = own_ref.shape[2]
    q = q_ref[0]
    for d, ref in enumerate((own_ref, r1_ref, r2_ref, r3_ref)):
        start = pl.multiple_of(lax.rem(q - d + GROUPS, GROUPS) * part, part)
        full_ref[:, :, pl.ds(start, part)] = ref[...]
    scatter_slots(loc_ref, count_ref, out_ref, lambda p: full_ref[p // loc_count])


def pack_gain_kernel(loc_count, loc_ref, taper_ref, own_ref, r1_ref, r2_ref, r3_ref, out_ref, full_ref, count_ref):
    full_ref[...] = (
        own_ref[...]
        + r1_ref[...].astype(jnp.float32)
        + r2_ref[...].astype(jnp.float32)
        + r3_ref[...].astype(jnp.float32)
    )
    scatter_slots(
        loc_ref,
        count_ref,
        out_ref,
        lambda p: (taper_ref[p] * full_ref[p // loc_count]).astype(out_ref.dtype),
    )


def pack(kernel, scalars, parts, full_dtype, members, tiles, slots):
    nblock, quarter, _ = parts[0].shape
    return pl.pallas_call(
        kernel,
        in_specs=[pl.BlockSpec(memory_space=pltpu.SMEM)] * len(scalars)
        + [pl.BlockSpec(memory_space=pltpu.VMEM)] * len(parts),
        out_specs=pl.BlockSpec(memory_space=pltpu.VMEM),
        out_shape=jax.ShapeDtypeStruct((slots, quarter, members), jnp.bfloat16),
        scratch_shapes=[
            pltpu.VMEM((nblock, quarter, members), full_dtype),
            pltpu.SMEM((tiles,), jnp.int32),
        ],
        compiler_params=pltpu.CompilerParams(vmem_limit_bytes=VMEM_LIMIT),
    )(*scalars, *parts)


def transform_kernel(q_ref, gain_ref, innov_ref, own_ref, s1_ref, s2_ref, s3_ref, total_ref):
    step = pl.program_id(0)
    part = own_ref.shape[1]

    @pl.when(step == 0)
    def _():
        total_ref[...] = jnp.zeros_like(total_ref)

    total_ref[...] += lax.dot_general(
        gain_ref[...], innov_ref[...], (((0,), (0,)), ((), ())), preferred_element_type=jnp.float32
    )

    @pl.when(step == pl.num_programs(0) - 1)
    def _():
        q = q_ref[0]
        for d, out_ref in enumerate((own_ref, s1_ref, s2_ref, s3_ref)):
            start = pl.multiple_of(lax.rem(q + d, GROUPS) * part, part)
            out_ref[...] = total_ref[:, pl.ds(start, part)].astype(out_ref.dtype)


def transform_parts(q, gain, innov):
    depth, members = gain.shape
    part = members // GROUPS
    step = 512
    out = pl.BlockSpec((members, part), lambda i, q: (0, 0))
    block = pl.BlockSpec((step, members), lambda i, q: (i, 0))
    return pl.pallas_call(
        transform_kernel,
        grid_spec=pltpu.PrefetchScalarGridSpec(
            num_scalar_prefetch=1,
            grid=(depth // step,),
            in_specs=[block, block],
            out_specs=[out] * GROUPS,
            scratch_shapes=[pltpu.VMEM((members, members), jnp.float32)],
        ),
        out_shape=[jax.ShapeDtypeStruct((members, part), jnp.float32)]
        + [jax.ShapeDtypeStruct((members, part), jnp.bfloat16)] * 3,
        compiler_params=pltpu.CompilerParams(vmem_limit_bytes=VMEM_LIMIT),
    )(q, gain, innov)


def update_kernel(
    order_ref, t0_ref, t1_ref, t2_ref, t3_ref, own_ref, a1_ref, a2_ref, b1_ref, b2_ref, o1_ref, o2_ref,
    out_ref, raw_ref, weights_ref, mean_ref, states_ref,
):
    step = pl.program_id(0)
    half = pl.num_programs(0) // 2
    part = own_ref.shape[1]
    members = t0_ref.shape[0]

    @pl.when(step == 0)
    def _():
        total = (
            t0_ref[...]
            + t1_ref[...].astype(jnp.float32)
            + t2_ref[...].astype(jnp.float32)
            + t3_ref[...].astype(jnp.float32)
        ).astype(jnp.bfloat16)
        raw_ref[...] = total.reshape(raw_ref.shape)
        mean_ref[...] = jnp.broadcast_to(
            jnp.sum(total.astype(jnp.float32), axis=0, keepdims=True) / members, mean_ref.shape
        )
        for k in range(GROUPS):
            weights_ref[pl.ds(k * part, part), :part] = raw_ref[order_ref[k]]
        weights_ref[:, part:] = jnp.ones((members, part), jnp.bfloat16)

    states_ref[:, :part] = own_ref[...]

    @pl.when(step < half)
    def _():
        for k, ref in enumerate((a1_ref, b1_ref, o1_ref)):
            states_ref[:, pl.ds((k + 1) * part, part)] = ref[...]

    @pl.when(step >= half)
    def _():
        for k, ref in enumerate((a2_ref, b2_ref, o2_ref)):
            states_ref[:, pl.ds((k + 1) * part, part)] = ref[...]

    both = jnp.dot(states_ref[...], weights_ref[...], preferred_element_type=jnp.float32)
    increment = (both[:, :part] - both[:, part:] * mean_ref[0:1, :]) * (1.0 / math.sqrt(members - 1))
    out_ref[...] = (own_ref[...].astype(jnp.float32) + increment).astype(out_ref.dtype)


def update(order, pieces, own, halves):
    rows, part = own.shape
    members = pieces[0].shape[0]
    half = 6
    step = rows // (2 * half)
    whole = pl.BlockSpec((members, part), lambda i, o: (0, 0))
    block = pl.BlockSpec((step, part), lambda i, o: (i, 0))
    low = pl.BlockSpec((step, part), lambda i, o: (jnp.minimum(i, half - 1), 0))
    high = pl.BlockSpec((step, part), lambda i, o: (jnp.maximum(i - half, 0), 0))
    return pl.pallas_call(
        update_kernel,
        grid_spec=pltpu.PrefetchScalarGridSpec(
            num_scalar_prefetch=1,
            grid=(2 * half,),
            in_specs=[whole] * 4 + [block] + [low, high] * 3,
            out_specs=block,
            scratch_shapes=[
                pltpu.VMEM((GROUPS, part, part), jnp.bfloat16),
                pltpu.VMEM((members, 2 * part), jnp.bfloat16),
                pltpu.VMEM((8, part), jnp.float32),
                pltpu.VMEM((step, members), jnp.bfloat16),
            ],
        ),
        out_shape=jax.ShapeDtypeStruct((rows, part), jnp.bfloat16),
        compiler_params=pltpu.CompilerParams(vmem_limit_bytes=VMEM_LIMIT),
    )(order, *pieces, own, *halves)


def shift(x, d):
    return lax.ppermute(x, "mem", [(i, (i + d) % GROUPS) for i in range(GROUPS)])


def swap_a(x):
    return lax.ppermute(x, "mem", [(0, 1), (1, 0), (2, 3), (3, 2)])


def swap_b(x):
    return lax.ppermute(x, "mem", [(0, 3), (3, 0), (1, 2), (2, 1)])


def per_device(
    ensemble, obs_anom, inverses, innovations, precision, obs_count, loc_tiles, taper_weight
):
    tiles = lax.axis_size("tile")
    nblock, obs_rows, part = obs_anom.shape
    members = part * GROUPS
    rows = ensemble.shape[0]
    loc_count = loc_tiles.shape[1]
    quarter = obs_rows // GROUPS
    slots = tiles * 2
    q = lax.axis_index("mem").astype(jnp.int32)
    q1 = q.reshape(1)
    order = jnp.stack([q, q ^ 1, 3 - q, q ^ 2])
    loc = loc_tiles.reshape(nblock * loc_count)
    taper = taper_weight.reshape(nblock * loc_count)

    g0, g1, g2, g3, w0, w1, w2, w3 = first_parts(
        q1, obs_anom, inverses, innovations, precision, obs_count
    )
    innov_parts = [w0, shift(w1, 1), shift(w2, 2), shift(w3, 3)]
    g1, g2, g3 = shift(g1, 1), shift(g2, 2), shift(g3, 3)
    g1, g2, g3, states = lax.optimization_barrier((g1, g2, g3, ensemble))

    low, high = states[: rows // 2], states[rows // 2 :]
    a1, b2 = swap_a(low), swap_b(high)
    a2, b1 = swap_a(high), swap_b(low)
    o1, o2 = swap_b(a1), swap_a(b2)

    send_innov = pack(
        functools.partial(pack_innov_kernel, loc_count), (q1, loc), innov_parts, jnp.bfloat16,
        members, tiles, slots,
    )
    recv_innov = lax.all_to_all(send_innov, "tile", split_axis=0, concat_axis=0, tiled=True)
    send_gain = pack(
        functools.partial(pack_gain_kernel, loc_count), (loc, taper), [g0, g1, g2, g3],
        jnp.float32, members, tiles, slots,
    )
    recv_gain = lax.all_to_all(send_gain, "tile", split_axis=0, concat_axis=0, tiled=True)
    t0, t1, t2, t3 = transform_parts(
        q1,
        recv_gain.reshape(slots * quarter, members),
        recv_innov.reshape(slots * quarter, members),
    )
    pieces = [t0, shift(t1, 1), shift(t2, 2), shift(t3, 3)]
    return update(order, pieces, ensemble, (a1, a2, b1, b2, o1, o2))


def solution(mesh):
    return jax.shard_map(
        per_device,
        mesh=mesh,
        in_specs=(
            P("tile", "mem"),
            P("tile", None, "mem"),
            P("tile", None, "mem"),
            P("tile", None, "mem"),
            P("tile", None),
            P("tile"),
            P("tile", None),
            P("tile", None),
        ),
        out_specs=P("tile", "mem"),
        check_vma=False,
    )
```

```python
import functools
import math

import jax
import jax.numpy as jnp
from jax import lax
from jax.experimental import pallas as pl
from jax.experimental.pallas import tpu as pltpu
from jax.sharding import PartitionSpec as P

VMEM_LIMIT = 56 * 1024 * 1024
GROUPS = 4


def first_kernel(
    q_ref, obs_ref, inv_ref, innov_ref, precision_ref, count_ref,
    gain_ref, innov_out_ref, m1_ref, m2_ref, m3_ref, rows_ref, live_ref,
):
    quarter, members = gain_ref.shape[1:]
    obs_rows, part = innov_ref.shape[1:]
    blocks = obs_ref.shape[0]
    q = q_ref[0]
    step = pl.program_id(0)
    position = lax.broadcasted_iota(jnp.int32, (obs_rows, part), 0)
    for k in range(blocks):
        rows_ref[...] = lax.dot_general(
            obs_ref[k], inv_ref[k], (((1,), (1,)), ((), ())), preferred_element_type=jnp.float32
        )
        block = step * blocks + k
        scale = jnp.broadcast_to(precision_ref[pl.ds(block, 1), :], (part, obs_rows)).T
        live_ref[...] = jnp.where(
            position < count_ref[block], scale * innov_ref[k].astype(jnp.float32), 0.0
        )
        own = pl.ds(pl.multiple_of(q * quarter, quarter), quarter)
        gain_ref[k] = rows_ref[own, :]
        innov_out_ref[k] = live_ref[own, :].astype(jnp.bfloat16)
        for d, ref in ((1, m1_ref), (2, m2_ref), (3, m3_ref)):
            rows = pl.ds(pl.multiple_of(lax.rem(q + d, GROUPS) * quarter, quarter), quarter)
            ref[k, :, :members] = rows_ref[rows, :].astype(jnp.bfloat16)
            ref[k, :, members:] = live_ref[rows, :].astype(jnp.bfloat16)


def first_parts(q, obs_anom, inverses, innovations, precision, obs_count):
    nblock, obs_rows, part = obs_anom.shape
    members = inverses.shape[1]
    quarter = obs_rows // GROUPS
    step = 4
    widths = [members, part] + [members + part] * 3
    types = [jnp.float32] + [jnp.bfloat16] * 4
    rows = pl.BlockSpec((step, obs_rows, part), lambda i, q: (i, 0, 0))
    return pl.pallas_call(
        first_kernel,
        grid_spec=pltpu.PrefetchScalarGridSpec(
            num_scalar_prefetch=1,
            grid=(nblock // step,),
            in_specs=[
                rows,
                pl.BlockSpec((step, members, part), lambda i, q: (i, 0, 0)),
                rows,
                pl.BlockSpec((nblock, obs_rows), lambda i, q: (0, 0)),
                pl.BlockSpec(memory_space=pltpu.SMEM),
            ],
            out_specs=[
                pl.BlockSpec((step, quarter, width), lambda i, q: (i, 0, 0)) for width in widths
            ],
            scratch_shapes=[
                pltpu.VMEM((obs_rows, members), jnp.float32),
                pltpu.VMEM((obs_rows, part), jnp.float32),
            ],
        ),
        out_shape=[
            jax.ShapeDtypeStruct((nblock, quarter, width), kind)
            for width, kind in zip(widths, types)
        ],
        compiler_params=pltpu.CompilerParams(vmem_limit_bytes=VMEM_LIMIT),
    )(q, obs_anom, inverses, innovations, precision, obs_count)


def pack_kernel(
    loc_count, q_ref, loc_ref, taper_ref, gain_ref, innov_ref, r1_ref, r2_ref, r3_ref,
    out_ref, gain_full_ref, innov_full_ref, count_ref,
):
    members = gain_ref.shape[2]
    part = innov_ref.shape[2]
    pairs = loc_ref.shape[0]
    tiles = count_ref.shape[0]
    capacity = out_ref.shape[0] // tiles
    q = q_ref[0]
    innov_full_ref[:, :, pl.ds(pl.multiple_of(q * part, part), part)] = innov_ref[...]
    for d, ref in ((1, r1_ref), (2, r2_ref), (3, r3_ref)):
        start = pl.multiple_of(lax.rem(q - d + GROUPS, GROUPS) * part, part)
        innov_full_ref[:, :, pl.ds(start, part)] = ref[:, :, members:]
    gain_full_ref[...] = (
        gain_ref[...]
        + r1_ref[:, :, :members].astype(jnp.float32)
        + r2_ref[:, :, :members].astype(jnp.float32)
        + r3_ref[:, :, :members].astype(jnp.float32)
    )
    out_ref[...] = jnp.zeros(out_ref.shape, out_ref.dtype)

    def clear(t, _):
        count_ref[t] = 0
        return 0

    def put(p, _):
        tile = loc_ref[p]
        block = p // loc_count
        rank = count_ref[tile]
        count_ref[tile] = rank + 1
        slot = tile * capacity + rank
        out_ref[slot, :, :members] = (taper_ref[p] * gain_full_ref[block]).astype(out_ref.dtype)
        out_ref[slot, :, members:] = innov_full_ref[block]
        return 0

    lax.fori_loop(0, tiles, clear, 0)
    lax.fori_loop(0, pairs, put, 0)


def pack(q, loc, taper, parts, tiles, slots, loc_count):
    nblock, quarter, members = parts[0].shape
    return pl.pallas_call(
        functools.partial(pack_kernel, loc_count),
        in_specs=[pl.BlockSpec(memory_space=pltpu.SMEM)] * 3
        + [pl.BlockSpec(memory_space=pltpu.VMEM)] * len(parts),
        out_specs=pl.BlockSpec(memory_space=pltpu.VMEM),
        out_shape=jax.ShapeDtypeStruct((slots, quarter, 2 * members), jnp.bfloat16),
        scratch_shapes=[
            pltpu.VMEM((nblock, quarter, members), jnp.float32),
            pltpu.VMEM((nblock, quarter, members), jnp.bfloat16),
            pltpu.SMEM((tiles,), jnp.int32),
        ],
        compiler_params=pltpu.CompilerParams(vmem_limit_bytes=VMEM_LIMIT),
    )(q, loc, taper, *parts)


def arrived_kernel(a1_ref, a2_ref, b1_ref, b2_ref, out_ref):
    out_ref[0] = 0


def arrived(*arrays):
    return pl.pallas_call(
        arrived_kernel,
        in_specs=[pl.BlockSpec(memory_space=pl.ANY)] * len(arrays),
        out_specs=pl.BlockSpec(memory_space=pltpu.SMEM),
        out_shape=jax.ShapeDtypeStruct((1,), jnp.int32),
        cost_estimate=pl.CostEstimate(flops=10**12, bytes_accessed=10**9, transcendentals=0),
    )(*arrays)


def transform_kernel(q_ref, token_ref, pairs_ref, own_ref, s1_ref, s2_ref, s3_ref, total_ref):
    step = pl.program_id(0)
    members, part = own_ref.shape

    @pl.when(step == 0)
    def _():
        total_ref[...] = jnp.zeros_like(total_ref)

    total_ref[...] += lax.dot_general(
        pairs_ref[:, :members],
        pairs_ref[:, members:],
        (((0,), (0,)), ((), ())),
        preferred_element_type=jnp.float32,
    )

    @pl.when(step == pl.num_programs(0) - 1)
    def _():
        q = q_ref[0]
        for d, out_ref in enumerate((own_ref, s1_ref, s2_ref, s3_ref)):
            start = pl.multiple_of(lax.rem(q + d, GROUPS) * part, part)
            columns = total_ref[:, pl.ds(start, part)]
            mean = jnp.sum(columns, axis=0, keepdims=True) / members
            scaled = (columns - mean) * (1.0 / math.sqrt(members - 1))
            out_ref[...] = scaled.astype(out_ref.dtype)


def transform_parts(q, token, pairs):
    depth, width = pairs.shape
    members = width // 2
    part = members // GROUPS
    step = 512
    out = pl.BlockSpec((members, part), lambda i, q, token: (0, 0))
    return pl.pallas_call(
        transform_kernel,
        grid_spec=pltpu.PrefetchScalarGridSpec(
            num_scalar_prefetch=2,
            grid=(depth // step,),
            in_specs=[pl.BlockSpec((step, width), lambda i, q, token: (i, 0))],
            out_specs=[out] * GROUPS,
            scratch_shapes=[pltpu.VMEM((members, members), jnp.float32)],
        ),
        out_shape=[jax.ShapeDtypeStruct((members, part), jnp.float32)]
        + [jax.ShapeDtypeStruct((members, part), jnp.bfloat16)] * 3,
        compiler_params=pltpu.CompilerParams(vmem_limit_bytes=VMEM_LIMIT),
    )(q, token, pairs)


def update_kernel(
    order_ref, t0_ref, t1_ref, t2_ref, t3_ref, own_ref, a1_ref, a2_ref, b1_ref, b2_ref, o1_ref, o2_ref,
    out_ref, raw_ref, weights_ref,
):
    step = pl.program_id(0)
    half = pl.num_programs(0) // 2
    part = own_ref.shape[1]

    @pl.when(step == 0)
    def _():
        total = (
            t0_ref[...]
            + t1_ref[...].astype(jnp.float32)
            + t2_ref[...].astype(jnp.float32)
            + t3_ref[...].astype(jnp.float32)
        ).astype(jnp.bfloat16)
        raw_ref[...] = total.reshape(raw_ref.shape)
        for k in range(GROUPS):
            weights_ref[pl.ds(k * part, part), :] = raw_ref[order_ref[k]]

    def rows(a_ref, b_ref, o_ref):
        own = own_ref[...]
        states = jnp.concatenate([own, a_ref[...], b_ref[...], o_ref[...]], axis=1)
        increment = jnp.dot(states, weights_ref[...], preferred_element_type=jnp.float32)
        out_ref[...] = (own.astype(jnp.float32) + increment).astype(out_ref.dtype)

    @pl.when(step < half)
    def _():
        rows(a1_ref, b1_ref, o1_ref)

    @pl.when(step >= half)
    def _():
        rows(a2_ref, b2_ref, o2_ref)


def update(order, pieces, own, halves):
    rows, part = own.shape
    members = pieces[0].shape[0]
    half = 3
    step = rows // (2 * half)
    whole = pl.BlockSpec((members, part), lambda i, o: (0, 0))
    block = pl.BlockSpec((step, part), lambda i, o: (i, 0))
    low = pl.BlockSpec((step, part), lambda i, o: (jnp.minimum(i, half - 1), 0))
    high = pl.BlockSpec((step, part), lambda i, o: (jnp.maximum(i - half, 0), 0))
    return pl.pallas_call(
        update_kernel,
        grid_spec=pltpu.PrefetchScalarGridSpec(
            num_scalar_prefetch=1,
            grid=(2 * half,),
            in_specs=[whole] * 4 + [block] + [low, high] * 3,
            out_specs=block,
            scratch_shapes=[
                pltpu.VMEM((GROUPS, part, part), jnp.bfloat16),
                pltpu.VMEM((members, part), jnp.bfloat16),
            ],
        ),
        out_shape=jax.ShapeDtypeStruct((rows, part), jnp.bfloat16),
        compiler_params=pltpu.CompilerParams(vmem_limit_bytes=VMEM_LIMIT),
    )(order, *pieces, own, *halves)


def shift(x, d):
    return lax.ppermute(x, "mem", [(i, (i + d) % GROUPS) for i in range(GROUPS)])


def swap_a(x):
    return lax.ppermute(x, "mem", [(0, 1), (1, 0), (2, 3), (3, 2)])


def swap_b(x):
    return lax.ppermute(x, "mem", [(0, 3), (3, 0), (1, 2), (2, 1)])


def per_device(
    ensemble, obs_anom, inverses, innovations, precision, obs_count, loc_tiles, taper_weight
):
    tiles = lax.axis_size("tile")
    nblock, obs_rows, part = obs_anom.shape
    members = part * GROUPS
    rows = ensemble.shape[0]
    loc_count = loc_tiles.shape[1]
    quarter = obs_rows // GROUPS
    slots = tiles * 2
    q = lax.axis_index("mem").astype(jnp.int32)
    q1 = q.reshape(1)
    order = jnp.stack([q, q ^ 1, 3 - q, q ^ 2])
    loc = loc_tiles.reshape(nblock * loc_count)
    taper = taper_weight.reshape(nblock * loc_count)

    gain, innov, m1, m2, m3 = first_parts(
        q1, obs_anom, inverses, innovations, precision, obs_count
    )
    m1, m2, m3 = shift(m1, 1), shift(m2, 2), shift(m3, 3)
    m1, m2, m3, low, high = lax.optimization_barrier(
        (m1, m2, m3, ensemble[: rows // 2], ensemble[rows // 2 :])
    )
    a1, b2 = swap_a(low), swap_b(high)
    a2, b1 = swap_a(high), swap_b(low)
    o1, o2 = swap_b(a1), swap_a(b2)

    send = pack(q1, loc, taper, (gain, innov, m1, m2, m3), tiles, slots, loc_count)
    received = lax.all_to_all(send, "tile", split_axis=0, concat_axis=0, tiled=True)
    token = arrived(a1, a2, b1, b2)
    t0, t1, t2, t3 = transform_parts(q1, token, received.reshape(slots * quarter, 2 * members))
    pieces = [t0, shift(t1, 1), shift(t2, 2), shift(t3, 3)]
    return update(order, pieces, ensemble, (a1, a2, b1, b2, o1, o2))


def solution(mesh):
    return jax.shard_map(
        per_device,
        mesh=mesh,
        in_specs=(
            P("tile", "mem"),
            P("tile", None, "mem"),
            P("tile", None, "mem"),
            P("tile", None, "mem"),
            P("tile", None),
            P("tile"),
            P("tile", None),
            P("tile", None),
        ),
        out_specs=P("tile", "mem"),
        check_vma=False,
    )
```

```python
import functools
import math

import jax
import jax.numpy as jnp
from jax import lax
from jax.experimental import pallas as pl
from jax.experimental.pallas import tpu as pltpu
from jax.sharding import PartitionSpec as P

VMEM_LIMIT = 24 * 1024 * 1024
FIRST_LIMIT = 60 * 1024 * 1024
GROUPS = 4
DEPTH = 8
CORES = 2
SLOTS = 2
STEPS = 6
SMALL = pl.CostEstimate(flops=10**6, bytes_accessed=10**6, transcendentals=0)


def first_kernel(
    q_ref, obs_ref, inv_ref, innov_ref, precision_ref, count_ref,
    gain_ref, innov_out_ref, m1_ref, m2_ref, m3_ref, rows_ref, live_ref,
):
    quarter, members = gain_ref.shape[1:]
    obs_rows, part = innov_ref.shape[1:]
    blocks = obs_ref.shape[0]
    q = q_ref[0]
    step = pl.program_id(0)
    position = lax.broadcasted_iota(jnp.int32, (obs_rows, part), 0)
    for k in range(blocks):
        rows_ref[...] = lax.dot_general(
            obs_ref[k], inv_ref[k], (((1,), (1,)), ((), ())), preferred_element_type=jnp.float32
        )
        block = step * blocks + k
        scale = jnp.broadcast_to(precision_ref[pl.ds(block, 1), :], (part, obs_rows)).T
        live_ref[...] = jnp.where(
            position < count_ref[block], scale * innov_ref[k].astype(jnp.float32), 0.0
        )
        own = pl.ds(pl.multiple_of(q * quarter, quarter), quarter)
        gain_ref[k] = rows_ref[own, :]
        innov_out_ref[k] = live_ref[own, :].astype(jnp.bfloat16)
        for d, ref in ((1, m1_ref), (2, m2_ref), (3, m3_ref)):
            rows = pl.ds(pl.multiple_of(lax.rem(q + d, GROUPS) * quarter, quarter), quarter)
            ref[k, :, :members] = rows_ref[rows, :].astype(jnp.bfloat16)
            ref[k, :, members:] = live_ref[rows, :].astype(jnp.bfloat16)


def first_parts(q, obs_anom, inverses, innovations, precision, obs_count):
    nblock, obs_rows, part = obs_anom.shape
    members = inverses.shape[1]
    quarter = obs_rows // GROUPS
    step = 4
    widths = [members, part] + [members + part] * 3
    types = [jnp.float32] + [jnp.bfloat16] * 4
    rows = pl.BlockSpec((step, obs_rows, part), lambda i, q: (i, 0, 0))
    return pl.pallas_call(
        first_kernel,
        grid_spec=pltpu.PrefetchScalarGridSpec(
            num_scalar_prefetch=1,
            grid=(nblock // step,),
            in_specs=[
                rows,
                pl.BlockSpec((step, members, part), lambda i, q: (i, 0, 0)),
                rows,
                pl.BlockSpec((nblock, obs_rows), lambda i, q: (0, 0)),
                pl.BlockSpec(memory_space=pltpu.SMEM),
            ],
            out_specs=[
                pl.BlockSpec((step, quarter, width), lambda i, q: (i, 0, 0)) for width in widths
            ],
            scratch_shapes=[
                pltpu.VMEM((obs_rows, members), jnp.float32),
                pltpu.VMEM((obs_rows, part), jnp.float32),
            ],
        ),
        out_shape=[
            jax.ShapeDtypeStruct((nblock, quarter, width), kind)
            for width, kind in zip(widths, types)
        ],
        compiler_params=pltpu.CompilerParams(vmem_limit_bytes=FIRST_LIMIT),
    )(q, obs_anom, inverses, innovations, precision, obs_count)


def merge_kernel(
    q_ref, chosen_ref, taper_ref, gain_ref, innov_ref, r1_ref, r2_ref, r3_ref, low_ref, high_ref
):
    members = gain_ref.shape[2]
    part = innov_ref.shape[2]
    half = high_ref.shape[0]
    q = q_ref[0]
    gain = (
        gain_ref[...]
        + r1_ref[:, :, :members].astype(jnp.float32)
        + r2_ref[:, :, :members].astype(jnp.float32)
        + r3_ref[:, :, :members].astype(jnp.float32)
    ).astype(jnp.bfloat16)
    for out_ref, blocks in ((low_ref, slice(0, half)), (high_ref, slice(half, 2 * half))):
        out_ref[:half, :, :members] = gain[blocks]
        start = pl.multiple_of(members + q * part, part)
        out_ref[:half, :, pl.ds(start, part)] = innov_ref[blocks]
        for d, ref in ((1, r1_ref), (2, r2_ref), (3, r3_ref)):
            start = pl.multiple_of(members + lax.rem(q - d + GROUPS, GROUPS) * part, part)
            out_ref[:half, :, pl.ds(start, part)] = ref[blocks, :, members:]
    lanes = chosen_ref.shape[1]
    low_ref[half] = jnp.zeros(low_ref.shape[1:], low_ref.dtype)
    quarter = low_ref.shape[1]
    rest = jnp.broadcast_to(taper_ref[...], (quarter, lanes))
    low_ref[half, :, :lanes] = jnp.broadcast_to(chosen_ref[...], (quarter, lanes)).astype(jnp.bfloat16)
    for k in range(1, 4):
        term = rest.astype(jnp.bfloat16)
        rest = rest - term.astype(jnp.float32)
        low_ref[half, :, k * lanes : (k + 1) * lanes] = term


def merge(q, chosen, taper, parts):
    nblock, quarter, members = parts[0].shape
    half = nblock // 2
    vmem = pl.BlockSpec(memory_space=pltpu.VMEM)
    return pl.pallas_call(
        merge_kernel,
        in_specs=[pl.BlockSpec(memory_space=pltpu.SMEM)] + [vmem] * (2 + len(parts)),
        out_specs=[vmem] * 2,
        out_shape=[
            jax.ShapeDtypeStruct((half + 1, quarter, 2 * members), jnp.bfloat16),
            jax.ShapeDtypeStruct((half, quarter, 2 * members), jnp.bfloat16),
        ],
        compiler_params=pltpu.CompilerParams(vmem_limit_bytes=VMEM_LIMIT),
        cost_estimate=SMALL,
    )(q, chosen, taper, *parts)


def sums_kernel(same, token_ref, place_ref, *refs):
    lows, highs, refs = refs[:DEPTH], refs[DEPTH : 2 * DEPTH], refs[2 * DEPTH :]
    others = ()
    if same:
        others, refs = refs[:GROUPS], refs[GROUPS:]
    outs, refs = refs[:GROUPS], refs[GROUPS:]
    all_ref, gain_ref, innov_ref, chosen_ref, taper_ref, chosen_smem, taper_smem, sems = refs
    half, quarter, width = highs[0].shape
    members = width // 2
    lanes = chosen_ref.shape[1]
    copies = []
    for k in range(DEPTH):
        copies.append(pltpu.make_async_copy(lows[k], all_ref.at[k, pl.ds(0, half + 1)], sems.at[2 * k]))
        copies.append(
            pltpu.make_async_copy(highs[k], all_ref.at[k, pl.ds(half + 1, half)], sems.at[2 * k + 1])
        )
    for copy in copies:
        copy.start()
    for k in range(DEPTH):
        copies[2 * k].wait()
        meta = all_ref[k, half, :, : 4 * lanes].astype(jnp.float32)[0:1]
        block = meta[:, :lanes].astype(jnp.int32)
        chosen_ref[pl.ds(k, 1), :] = block + jnp.where(block < half, 0, 1)
        taper_ref[pl.ds(k, 1), :] = (
            meta[:, lanes : 2 * lanes] + meta[:, 2 * lanes : 3 * lanes] + meta[:, 3 * lanes :]
        )
    tables = [
        pltpu.make_async_copy(chosen_ref, chosen_smem, sems.at[2 * DEPTH]),
        pltpu.make_async_copy(taper_ref, taper_smem, sems.at[2 * DEPTH + 1]),
    ]
    for copy in tables:
        copy.start()
    for k in range(DEPTH):
        copies[2 * k + 1].wait()
    for copy in tables:
        copy.wait()
    core = place_ref[2] if same else 1 - place_ref[2]
    for away in range(GROUPS):
        column = lax.rem(place_ref[0] + away, GROUPS)
        tile = (column * DEPTH + place_ref[1]) * CORES + core
        for k in range(DEPTH):
            for r in range(SLOTS):
                entry = r * (lanes // SLOTS) + tile
                block = chosen_smem[k, entry]
                rows = pl.ds((k * SLOTS + r) * quarter, quarter)
                gain = all_ref[k, block, :, :members].astype(jnp.float32)
                gain_ref[away, rows, :] = (taper_smem[k, entry] * gain).astype(jnp.bfloat16)
                innov_ref[away, rows, :] = all_ref[k, block, :, members:]
        total = lax.dot_general(
            gain_ref[away],
            innov_ref[away],
            (((0,), (0,)), ((), ())),
            preferred_element_type=jnp.float32,
        )
        if same:
            total = total + others[away][...].astype(jnp.float32)
        outs[away][...] = total.astype(outs[away].dtype)


def sums(same, token, place, lows, highs, others=()):
    half, quarter, width = highs[0].shape
    members = width // 2
    lanes = 128
    kinds = [jnp.float32 if same else jnp.bfloat16] + [jnp.bfloat16] * (GROUPS - 1)
    taken = (GROUPS, DEPTH * SLOTS * quarter, members)
    return pl.pallas_call(
        functools.partial(sums_kernel, same),
        in_specs=[pl.BlockSpec(memory_space=pltpu.SMEM)] * 2
        + [pl.BlockSpec(memory_space=pl.ANY)] * (2 * DEPTH)
        + [pl.BlockSpec(memory_space=pltpu.VMEM)] * len(others),
        out_specs=[pl.BlockSpec(memory_space=pltpu.VMEM)] * GROUPS,
        out_shape=[jax.ShapeDtypeStruct((members, members), kind) for kind in kinds],
        scratch_shapes=[
            pltpu.VMEM((DEPTH, 2 * half + 1, quarter, width), jnp.bfloat16),
            pltpu.VMEM(taken, jnp.bfloat16),
            pltpu.VMEM(taken, jnp.bfloat16),
            pltpu.VMEM((DEPTH, lanes), jnp.int32),
            pltpu.VMEM((DEPTH, lanes), jnp.float32),
            pltpu.SMEM((DEPTH, lanes), jnp.int32),
            pltpu.SMEM((DEPTH, lanes), jnp.float32),
            pltpu.SemaphoreType.DMA((2 * DEPTH + 2,)),
        ],
        compiler_params=pltpu.CompilerParams(vmem_limit_bytes=VMEM_LIMIT),
        cost_estimate=SMALL,
    )(token, place, *lows, *highs, *others)


def arrived_kernel(*refs):
    refs[-1][0] = 0


def arrived(*arrays):
    return pl.pallas_call(
        arrived_kernel,
        in_specs=[pl.BlockSpec(memory_space=pl.ANY)] * len(arrays),
        out_specs=pl.BlockSpec(memory_space=pltpu.SMEM),
        out_shape=jax.ShapeDtypeStruct((1,), jnp.int32),
        cost_estimate=pl.CostEstimate(flops=10**12, bytes_accessed=10**9, transcendentals=0),
    )(*arrays)


def transform_kernel(q_ref, token_ref, r0_ref, r1_ref, r2_ref, r3_ref, own_ref, s1_ref, s2_ref, s3_ref):
    q = q_ref[0]
    members, part = own_ref.shape
    for d, out_ref in enumerate((own_ref, s1_ref, s2_ref, s3_ref)):
        columns = pl.ds(pl.multiple_of(lax.rem(q + d, GROUPS) * part, part), part)
        total = (
            r0_ref[:, columns]
            + r1_ref[:, columns].astype(jnp.float32)
            + r2_ref[:, columns].astype(jnp.float32)
            + r3_ref[:, columns].astype(jnp.float32)
        )
        mean = jnp.sum(total, axis=0, keepdims=True) / members
        out_ref[...] = ((total - mean) * (1.0 / math.sqrt(members - 1))).astype(out_ref.dtype)


def transform_parts(q, token, sums_here):
    members = sums_here[0].shape[0]
    part = members // GROUPS
    return pl.pallas_call(
        transform_kernel,
        in_specs=[pl.BlockSpec(memory_space=pltpu.SMEM)] * 2
        + [pl.BlockSpec(memory_space=pltpu.VMEM)] * GROUPS,
        out_specs=[pl.BlockSpec(memory_space=pltpu.VMEM)] * GROUPS,
        out_shape=[jax.ShapeDtypeStruct((members, part), jnp.float32)]
        + [jax.ShapeDtypeStruct((members, part), jnp.bfloat16)] * 3,
        compiler_params=pltpu.CompilerParams(vmem_limit_bytes=VMEM_LIMIT),
        cost_estimate=SMALL,
    )(q, token, *sums_here)


def update_kernel(
    order_ref, t0_ref, t1_ref, t2_ref, t3_ref, own_ref, a1_ref, a2_ref, b1_ref, b2_ref, o1_ref, o2_ref,
    out_ref, raw_ref, weights_ref, states_ref, result_ref, in_sems, out_sems,
):
    part = own_ref.shape[1]
    step = result_ref.shape[1]
    half = STEPS // 2
    loads = []
    for i in range(STEPS):
        sources = (a1_ref, b1_ref, o1_ref) if i < half else (a2_ref, b2_ref, o2_ref)
        views = [own_ref.at[pl.ds(i * step, step)]]
        views += [ref.at[pl.ds((i % half) * step, step)] for ref in sources]
        loads.append(
            [
                pltpu.make_async_copy(view, states_ref.at[i, k], in_sems.at[i, k])
                for k, view in enumerate(views)
            ]
        )
        for load in loads[-1]:
            load.start()
    total = (
        t0_ref[...]
        + t1_ref[...].astype(jnp.float32)
        + t2_ref[...].astype(jnp.float32)
        + t3_ref[...].astype(jnp.float32)
    ).astype(jnp.bfloat16)
    raw_ref[...] = total.reshape(raw_ref.shape)
    for k in range(GROUPS):
        weights_ref[pl.ds(k * part, part), :] = raw_ref[order_ref[k]]
    stores = []
    for i in range(STEPS):
        for load in loads[i]:
            load.wait()
        states = jnp.concatenate([states_ref[i, k] for k in range(GROUPS)], axis=1)
        increment = jnp.dot(states, weights_ref[...], preferred_element_type=jnp.float32)
        result_ref[i] = (states_ref[i, 0].astype(jnp.float32) + increment).astype(result_ref.dtype)
        stores.append(
            pltpu.make_async_copy(
                result_ref.at[i], out_ref.at[pl.ds(i * step, step)], out_sems.at[i]
            )
        )
        stores[-1].start()
    for store in stores:
        store.wait()


def update(order, pieces, own, others):
    rows, part = own.shape
    members = pieces[0].shape[0]
    step = rows // STEPS
    return pl.pallas_call(
        update_kernel,
        in_specs=[pl.BlockSpec(memory_space=pltpu.SMEM)]
        + [pl.BlockSpec(memory_space=pltpu.VMEM)] * GROUPS
        + [pl.BlockSpec(memory_space=pl.ANY)] * (1 + len(others)),
        out_specs=pl.BlockSpec(memory_space=pl.ANY),
        out_shape=jax.ShapeDtypeStruct((rows, part), jnp.bfloat16),
        scratch_shapes=[
            pltpu.VMEM((GROUPS, part, part), jnp.bfloat16),
            pltpu.VMEM((members, part), jnp.bfloat16),
            pltpu.VMEM((STEPS, GROUPS, step, part), jnp.bfloat16),
            pltpu.VMEM((STEPS, step, part), jnp.bfloat16),
            pltpu.SemaphoreType.DMA((STEPS, GROUPS)),
            pltpu.SemaphoreType.DMA((STEPS,)),
        ],
        compiler_params=pltpu.CompilerParams(vmem_limit_bytes=FIRST_LIMIT),
    )(order, *pieces, own, *others)


def shift(x, d):
    return lax.ppermute(x, "mem", [(i, (i + d) % GROUPS) for i in range(GROUPS)])


def swap_a(x):
    return lax.ppermute(x, "mem", [(0, 1), (1, 0), (2, 3), (3, 2)])


def swap_b(x):
    return lax.ppermute(x, "mem", [(0, 3), (3, 0), (1, 2), (2, 1)])


def move(x, columns, away=(0, 0, 0)):
    pairs = []
    for c in range(columns):
        for z in range(DEPTH):
            for k in range(CORES):
                target = (c + away[0]) % columns, (z + away[1]) % DEPTH, (k + away[2]) % CORES
                pairs.append(
                    ((c * DEPTH + z) * CORES + k, (target[0] * DEPTH + target[1]) * CORES + target[2])
                )
    return lax.ppermute(x, "tile", pairs)


def per_device(
    ensemble, obs_anom, inverses, innovations, precision, obs_count, loc_tiles, taper_weight
):
    columns = lax.axis_size("tile") // (DEPTH * CORES)
    nblock = obs_anom.shape[0]
    rows = ensemble.shape[0]
    loc_count = loc_tiles.shape[1]
    pairs = nblock * loc_count
    q = lax.axis_index("mem").astype(jnp.int32)
    q1 = q.reshape(1)
    order = jnp.stack([q, q ^ 1, 3 - q, q ^ 2])
    tile = lax.axis_index("tile").astype(jnp.int32)
    place = jnp.stack([tile // (DEPTH * CORES), (tile // CORES) & (DEPTH - 1), tile & (CORES - 1)])

    gain, innov, m1, m2, m3 = first_parts(
        q1, obs_anom, inverses, innovations, precision, obs_count
    )
    m1, m2, m3 = shift(m1, 1), shift(m2, 2), shift(m3, 3)

    tiles = columns * DEPTH * CORES
    loc = loc_tiles.reshape(pairs, 1)
    hits = (loc == lax.broadcasted_iota(jnp.int32, (pairs, tiles), 1)).astype(jnp.float32)
    same_tile = (loc == loc_tiles.reshape(1, pairs)).astype(jnp.float32)
    pair_at = lax.broadcasted_iota(jnp.int32, (pairs, 1), 0)
    earlier = (lax.broadcasted_iota(jnp.int32, (pairs, pairs), 1) < pair_at).astype(jnp.float32)
    rank = jnp.sum(same_tile * earlier, axis=1, keepdims=True)
    ranked = jnp.concatenate([hits * (rank == r).astype(jnp.float32) for r in range(SLOTS)], axis=1)
    block_of = (pair_at // loc_count).astype(jnp.float32)
    chosen = jnp.sum(ranked * block_of, axis=0, keepdims=True)
    tapers = jnp.sum(ranked * taper_weight.reshape(pairs, 1), axis=0, keepdims=True)

    half = rows // 2
    chosen, tapers, m1, m2, m3, low, high = lax.optimization_barrier(
        (chosen, tapers, m1, m2, m3, ensemble[:half], ensemble[half:])
    )
    a1, b2 = swap_a(low), swap_b(high)
    a2, b1 = swap_a(high), swap_b(low)
    o1, o2 = swap_b(a1), swap_a(b2)

    up, down = (0, 1, 0), (0, -1, 0)
    own_blocks = tuple(merge(q1, chosen, tapers, (gain, innov, m1, m2, m3)))
    ups, downs = [own_blocks], [own_blocks]
    for _ in range(3):
        ups.append(tuple(move(x, columns, up) for x in ups[-1]))
        downs.append(tuple(move(x, columns, down) for x in downs[-1]))
    far = (move(ups[-1][0], columns, up), move(downs[-1][1], columns, down))
    held = ups + downs[1:] + [far]
    lows, highs = [h[0] for h in held], [h[1] for h in held]
    token = arrived(a1, b2, *far)
    others = sums(0, token, place, lows, highs)
    others = [move(x, columns, (0, 0, 1)) for x in others]
    here, e1, e2, e3 = sums(1, token, place, lows, highs, others)
    e1, e2, e3 = move(e1, columns, (1, 0, 0)), move(e2, columns, (2, 0, 0)), move(e3, columns, (3, 0, 0))
    token = arrived(a2, b1, e1, e2, e3)
    t0, t1, t2, t3 = transform_parts(q1, token, (here, e1, e2, e3))
    pieces = [t0, shift(t1, 1), shift(t2, 2), shift(t3, 3)]
    return update(order, pieces, ensemble, (a1, a2, b1, b2, o1, o2))


def solution(mesh):
    return jax.shard_map(
        per_device,
        mesh=mesh,
        in_specs=(
            P("tile", "mem"),
            P("tile", None, "mem"),
            P("tile", None, "mem"),
            P("tile", None, "mem"),
            P("tile", None),
            P("tile"),
            P("tile", None),
            P("tile", None),
        ),
        out_specs=P("tile", "mem"),
        check_vma=False,
    )
```

```python
import functools
import math

import jax
import jax.numpy as jnp
from jax import lax
from jax.experimental import pallas as pl
from jax.experimental.pallas import tpu as pltpu
from jax.sharding import PartitionSpec as P

VMEM_LIMIT = 24 * 1024 * 1024
FIRST_LIMIT = 60 * 1024 * 1024
GROUPS = 4
DEPTH = 8
CORES = 2
SLOTS = 2
STEPS = 4
SMALL = pl.CostEstimate(flops=10**6, bytes_accessed=10**6, transcendentals=0)


def first_kernel(
    q_ref, obs_ref, inv_ref, innov_ref, precision_ref, count_ref,
    gain_ref, innov_out_ref, m1_ref, m2_ref, m3_ref, rows_ref, live_ref,
):
    quarter, members = gain_ref.shape[1:]
    obs_rows, part = innov_ref.shape[1:]
    blocks = obs_ref.shape[0]
    q = q_ref[0]
    step = pl.program_id(0)
    position = lax.broadcasted_iota(jnp.int32, (obs_rows, part), 0)
    for k in range(blocks):
        rows_ref[...] = lax.dot_general(
            obs_ref[k], inv_ref[k], (((1,), (1,)), ((), ())), preferred_element_type=jnp.float32
        )
        block = step * blocks + k
        scale = jnp.broadcast_to(precision_ref[pl.ds(block, 1), :], (part, obs_rows)).T
        live_ref[...] = jnp.where(
            position < count_ref[block], scale * innov_ref[k].astype(jnp.float32), 0.0
        )
        own = pl.ds(pl.multiple_of(q * quarter, quarter), quarter)
        gain_ref[k] = rows_ref[own, :]
        innov_out_ref[k] = live_ref[own, :].astype(jnp.bfloat16)
        for d, ref in ((1, m1_ref), (2, m2_ref), (3, m3_ref)):
            rows = pl.ds(pl.multiple_of(lax.rem(q + d, GROUPS) * quarter, quarter), quarter)
            ref[k, :, :members] = rows_ref[rows, :].astype(jnp.bfloat16)
            ref[k, :, members:] = live_ref[rows, :].astype(jnp.bfloat16)


def first_parts(q, obs_anom, inverses, innovations, precision, obs_count):
    nblock, obs_rows, part = obs_anom.shape
    members = inverses.shape[1]
    quarter = obs_rows // GROUPS
    step = 4
    widths = [members, part] + [members + part] * 3
    types = [jnp.float32] + [jnp.bfloat16] * 4
    rows = pl.BlockSpec((step, obs_rows, part), lambda i, q: (i, 0, 0))
    return pl.pallas_call(
        first_kernel,
        grid_spec=pltpu.PrefetchScalarGridSpec(
            num_scalar_prefetch=1,
            grid=(nblock // step,),
            in_specs=[
                rows,
                pl.BlockSpec((step, members, part), lambda i, q: (i, 0, 0)),
                rows,
                pl.BlockSpec((nblock, obs_rows), lambda i, q: (0, 0)),
                pl.BlockSpec(memory_space=pltpu.SMEM),
            ],
            out_specs=[
                pl.BlockSpec((step, quarter, width), lambda i, q: (i, 0, 0)) for width in widths
            ],
            scratch_shapes=[
                pltpu.VMEM((obs_rows, members), jnp.float32),
                pltpu.VMEM((obs_rows, part), jnp.float32),
            ],
        ),
        out_shape=[
            jax.ShapeDtypeStruct((nblock, quarter, width), kind)
            for width, kind in zip(widths, types)
        ],
        compiler_params=pltpu.CompilerParams(vmem_limit_bytes=FIRST_LIMIT),
    )(q, obs_anom, inverses, innovations, precision, obs_count)


def merge_kernel(
    q_ref, chosen_ref, taper_ref, gain_ref, innov_ref, r1_ref, r2_ref, r3_ref, low_ref, high_ref
):
    members = gain_ref.shape[2]
    part = innov_ref.shape[2]
    half = high_ref.shape[0]
    q = q_ref[0]
    gain = (
        gain_ref[...]
        + r1_ref[:, :, :members].astype(jnp.float32)
        + r2_ref[:, :, :members].astype(jnp.float32)
        + r3_ref[:, :, :members].astype(jnp.float32)
    ).astype(jnp.bfloat16)
    for out_ref, blocks in ((low_ref, slice(0, half)), (high_ref, slice(half, 2 * half))):
        out_ref[:half, :, :members] = gain[blocks]
        start = pl.multiple_of(members + q * part, part)
        out_ref[:half, :, pl.ds(start, part)] = innov_ref[blocks]
        for d, ref in ((1, r1_ref), (2, r2_ref), (3, r3_ref)):
            start = pl.multiple_of(members + lax.rem(q - d + GROUPS, GROUPS) * part, part)
            out_ref[:half, :, pl.ds(start, part)] = ref[blocks, :, members:]
    lanes = chosen_ref.shape[1]
    low_ref[half] = jnp.zeros(low_ref.shape[1:], low_ref.dtype)
    quarter = low_ref.shape[1]
    rest = jnp.broadcast_to(taper_ref[...], (quarter, lanes))
    low_ref[half, :, :lanes] = jnp.broadcast_to(chosen_ref[...], (quarter, lanes)).astype(jnp.bfloat16)
    for k in range(1, 4):
        term = rest.astype(jnp.bfloat16)
        rest = rest - term.astype(jnp.float32)
        low_ref[half, :, k * lanes : (k + 1) * lanes] = term


def merge(q, chosen, taper, parts):
    nblock, quarter, members = parts[0].shape
    half = nblock // 2
    vmem = pl.BlockSpec(memory_space=pltpu.VMEM)
    return pl.pallas_call(
        merge_kernel,
        in_specs=[pl.BlockSpec(memory_space=pltpu.SMEM)] + [vmem] * (2 + len(parts)),
        out_specs=[vmem] * 2,
        out_shape=[
            jax.ShapeDtypeStruct((half + 1, quarter, 2 * members), jnp.bfloat16),
            jax.ShapeDtypeStruct((half, quarter, 2 * members), jnp.bfloat16),
        ],
        compiler_params=pltpu.CompilerParams(vmem_limit_bytes=VMEM_LIMIT),
        cost_estimate=SMALL,
    )(q, chosen, taper, *parts)


def sums_kernel(same, token_ref, place_ref, *refs):
    lows, highs, refs = refs[:DEPTH], refs[DEPTH : 2 * DEPTH], refs[2 * DEPTH :]
    others, outs = (), ()
    if same:
        others, outs, refs = refs[:CORES], refs[CORES : CORES + GROUPS], refs[CORES + GROUPS :]
    else:
        outs, refs = refs[:CORES], refs[CORES:]
    pack = GROUPS // CORES
    all_ref, gain_ref, innov_ref, chosen_ref, taper_ref, chosen_smem, taper_smem, sems = refs
    half, quarter, width = highs[0].shape
    members = width // 2
    lanes = chosen_ref.shape[1]
    copies = []
    for k in range(DEPTH):
        copies.append(pltpu.make_async_copy(lows[k], all_ref.at[k, pl.ds(0, half + 1)], sems.at[2 * k]))
        copies.append(
            pltpu.make_async_copy(highs[k], all_ref.at[k, pl.ds(half + 1, half)], sems.at[2 * k + 1])
        )
    for copy in copies:
        copy.start()
    for k in range(DEPTH):
        copies[2 * k].wait()
        meta = all_ref[k, half, :, : 4 * lanes].astype(jnp.float32)[0:1]
        block = meta[:, :lanes].astype(jnp.int32)
        chosen_ref[pl.ds(k, 1), :] = block + jnp.where(block < half, 0, 1)
        taper_ref[pl.ds(k, 1), :] = (
            meta[:, lanes : 2 * lanes] + meta[:, 2 * lanes : 3 * lanes] + meta[:, 3 * lanes :]
        )
    tables = [
        pltpu.make_async_copy(chosen_ref, chosen_smem, sems.at[2 * DEPTH]),
        pltpu.make_async_copy(taper_ref, taper_smem, sems.at[2 * DEPTH + 1]),
    ]
    for copy in tables:
        copy.start()
    for k in range(DEPTH):
        copies[2 * k + 1].wait()
    for copy in tables:
        copy.wait()
    core = place_ref[2] if same else 1 - place_ref[2]
    for away in range(GROUPS):
        column = lax.rem(place_ref[0] + away, GROUPS)
        tile = (column * DEPTH + place_ref[1]) * CORES + core
        for k in range(DEPTH):
            for r in range(SLOTS):
                entry = r * (lanes // SLOTS) + tile
                block = chosen_smem[k, entry]
                rows = pl.ds((k * SLOTS + r) * quarter, quarter)
                gain = all_ref[k, block, :, :members].astype(jnp.float32)
                gain_ref[away, rows, :] = (taper_smem[k, entry] * gain).astype(jnp.bfloat16)
                innov_ref[away, rows, :] = all_ref[k, block, :, members:]
        total = lax.dot_general(
            gain_ref[away],
            innov_ref[away],
            (((0,), (0,)), ((), ())),
            preferred_element_type=jnp.float32,
        )
        if same:
            total = total + others[away // pack][away % pack].astype(jnp.float32)
            outs[away][...] = total.astype(outs[away].dtype)
        else:
            outs[away // pack][away % pack] = total.astype(jnp.bfloat16)


def sums(same, token, place, lows, highs, others=()):
    half, quarter, width = highs[0].shape
    members = width // 2
    lanes = 128
    square = (members, members)
    if same:
        kinds = [jnp.float32] + [jnp.bfloat16] * (GROUPS - 1)
        out_shape = [jax.ShapeDtypeStruct(square, kind) for kind in kinds]
    else:
        shape = (GROUPS // CORES,) + square
        out_shape = [jax.ShapeDtypeStruct(shape, jnp.bfloat16)] * CORES
    taken = (GROUPS, DEPTH * SLOTS * quarter, members)
    return pl.pallas_call(
        functools.partial(sums_kernel, same),
        in_specs=[pl.BlockSpec(memory_space=pltpu.SMEM)] * 2
        + [pl.BlockSpec(memory_space=pl.ANY)] * (2 * DEPTH)
        + [pl.BlockSpec(memory_space=pltpu.VMEM)] * len(others),
        out_specs=[pl.BlockSpec(memory_space=pltpu.VMEM)] * len(out_shape),
        out_shape=out_shape,
        scratch_shapes=[
            pltpu.VMEM((DEPTH, 2 * half + 1, quarter, width), jnp.bfloat16),
            pltpu.VMEM(taken, jnp.bfloat16),
            pltpu.VMEM(taken, jnp.bfloat16),
            pltpu.VMEM((DEPTH, lanes), jnp.int32),
            pltpu.VMEM((DEPTH, lanes), jnp.float32),
            pltpu.SMEM((DEPTH, lanes), jnp.int32),
            pltpu.SMEM((DEPTH, lanes), jnp.float32),
            pltpu.SemaphoreType.DMA((2 * DEPTH + 2,)),
        ],
        compiler_params=pltpu.CompilerParams(vmem_limit_bytes=VMEM_LIMIT),
        cost_estimate=SMALL,
    )(token, place, *lows, *highs, *others)


def arrived_kernel(*refs):
    refs[-1][0] = 0


def arrived(*arrays):
    return pl.pallas_call(
        arrived_kernel,
        in_specs=[pl.BlockSpec(memory_space=pl.ANY)] * len(arrays),
        out_specs=pl.BlockSpec(memory_space=pltpu.SMEM),
        out_shape=jax.ShapeDtypeStruct((1,), jnp.int32),
        cost_estimate=pl.CostEstimate(flops=10**12, bytes_accessed=10**9, transcendentals=0),
    )(*arrays)


def transform_kernel(q_ref, token_ref, r0_ref, r1_ref, r2_ref, r3_ref, own_ref, s1_ref, s2_ref, s3_ref):
    q = q_ref[0]
    members, part = own_ref.shape
    for d, out_ref in enumerate((own_ref, s1_ref, s2_ref, s3_ref)):
        columns = pl.ds(pl.multiple_of(lax.rem(q + d, GROUPS) * part, part), part)
        total = (
            r0_ref[:, columns]
            + r1_ref[:, columns].astype(jnp.float32)
            + r2_ref[:, columns].astype(jnp.float32)
            + r3_ref[:, columns].astype(jnp.float32)
        )
        mean = jnp.sum(total, axis=0, keepdims=True) / members
        out_ref[...] = ((total - mean) * (1.0 / math.sqrt(members - 1))).astype(out_ref.dtype)


def transform_parts(q, token, sums_here):
    members = sums_here[0].shape[0]
    part = members // GROUPS
    return pl.pallas_call(
        transform_kernel,
        in_specs=[pl.BlockSpec(memory_space=pltpu.SMEM)] * 2
        + [pl.BlockSpec(memory_space=pltpu.VMEM)] * GROUPS,
        out_specs=[pl.BlockSpec(memory_space=pltpu.VMEM)] * GROUPS,
        out_shape=[jax.ShapeDtypeStruct((members, part), jnp.float32)]
        + [jax.ShapeDtypeStruct((members, part), jnp.bfloat16)] * 3,
        compiler_params=pltpu.CompilerParams(vmem_limit_bytes=VMEM_LIMIT),
        cost_estimate=pl.CostEstimate(flops=5*10**9, bytes_accessed=10**6, transcendentals=0),
    )(q, token, *sums_here)


def hold_kernel(own_ref, a1_ref, a2_ref, b1_ref, b2_ref, out_ref, sems):
    half = a1_ref.shape[0]
    copies = [pltpu.make_async_copy(own_ref, out_ref.at[0], sems.at[0])]
    for k, (low, high) in enumerate(((a1_ref, a2_ref), (b1_ref, b2_ref))):
        copies.append(
            pltpu.make_async_copy(low, out_ref.at[k + 1, pl.ds(0, half)], sems.at[2 * k + 1])
        )
        copies.append(
            pltpu.make_async_copy(high, out_ref.at[k + 1, pl.ds(half, half)], sems.at[2 * k + 2])
        )
    for copy in copies:
        copy.start()
    for copy in copies:
        copy.wait()


def hold(own, others):
    rows, part = own.shape
    return pl.pallas_call(
        hold_kernel,
        in_specs=[pl.BlockSpec(memory_space=pl.ANY)] * (1 + len(others)),
        out_specs=pl.BlockSpec(memory_space=pltpu.VMEM),
        out_shape=jax.ShapeDtypeStruct((GROUPS - 1, rows, part), jnp.bfloat16),
        scratch_shapes=[pltpu.SemaphoreType.DMA((5,))],
        compiler_params=pltpu.CompilerParams(vmem_limit_bytes=16 * 1024 * 1024),
        cost_estimate=SMALL,
    )(own, *others)


def update_kernel(
    order_ref, t0_ref, t1_ref, t2_ref, t3_ref, held_ref, o1_ref, o2_ref,
    out_ref, raw_ref, weights_ref, far_ref, result_ref, in_sems, out_sems,
):
    part = held_ref.shape[2]
    step = result_ref.shape[1]
    half = STEPS // 2
    loads = []
    for i in range(STEPS):
        ref = o1_ref if i < half else o2_ref
        loads.append(
            pltpu.make_async_copy(ref.at[pl.ds((i % half) * step, step)], far_ref.at[i], in_sems.at[i])
        )
        loads[-1].start()
    total = (
        t0_ref[...]
        + t1_ref[...].astype(jnp.float32)
        + t2_ref[...].astype(jnp.float32)
        + t3_ref[...].astype(jnp.float32)
    ).astype(jnp.bfloat16)
    raw_ref[...] = total.reshape(raw_ref.shape)
    for k in range(GROUPS):
        weights_ref[pl.ds(k * part, part), :] = raw_ref[order_ref[k]]
    stores = []
    for i in range(STEPS):
        loads[i].wait()
        rows = pl.ds(i * step, step)
        near = [held_ref[k, rows, :] for k in range(GROUPS - 1)]
        states = jnp.concatenate(near + [far_ref[i]], axis=1)
        increment = jnp.dot(states, weights_ref[...], preferred_element_type=jnp.float32)
        result_ref[i] = (near[0].astype(jnp.float32) + increment).astype(result_ref.dtype)
        stores.append(pltpu.make_async_copy(result_ref.at[i], out_ref.at[rows], out_sems.at[i]))
        stores[-1].start()
    for store in stores:
        store.wait()


def update(order, pieces, held, others):
    rows, part = held.shape[1:]
    members = pieces[0].shape[0]
    step = rows // STEPS
    return pl.pallas_call(
        update_kernel,
        in_specs=[pl.BlockSpec(memory_space=pltpu.SMEM)]
        + [pl.BlockSpec(memory_space=pltpu.VMEM)] * (GROUPS + 1)
        + [pl.BlockSpec(memory_space=pl.ANY)] * len(others),
        out_specs=pl.BlockSpec(memory_space=pl.ANY),
        out_shape=jax.ShapeDtypeStruct((rows, part), jnp.bfloat16),
        scratch_shapes=[
            pltpu.VMEM((GROUPS, part, part), jnp.bfloat16),
            pltpu.VMEM((members, part), jnp.bfloat16),
            pltpu.VMEM((STEPS, step, part), jnp.bfloat16),
            pltpu.VMEM((STEPS, step, part), jnp.bfloat16),
            pltpu.SemaphoreType.DMA((STEPS,)),
            pltpu.SemaphoreType.DMA((STEPS,)),
        ],
        compiler_params=pltpu.CompilerParams(vmem_limit_bytes=VMEM_LIMIT),
    )(order, *pieces, held, *others)


def shift(x, d):
    return lax.ppermute(x, "mem", [(i, (i + d) % GROUPS) for i in range(GROUPS)])


def swap_a(x):
    return lax.ppermute(x, "mem", [(0, 1), (1, 0), (2, 3), (3, 2)])


def swap_b(x):
    return lax.ppermute(x, "mem", [(0, 3), (3, 0), (1, 2), (2, 1)])


def move(x, columns, away=(0, 0, 0)):
    pairs = []
    for c in range(columns):
        for z in range(DEPTH):
            for k in range(CORES):
                target = (c + away[0]) % columns, (z + away[1]) % DEPTH, (k + away[2]) % CORES
                pairs.append(
                    ((c * DEPTH + z) * CORES + k, (target[0] * DEPTH + target[1]) * CORES + target[2])
                )
    return lax.ppermute(x, "tile", pairs)


def per_device(
    ensemble, obs_anom, inverses, innovations, precision, obs_count, loc_tiles, taper_weight
):
    columns = lax.axis_size("tile") // (DEPTH * CORES)
    nblock = obs_anom.shape[0]
    rows = ensemble.shape[0]
    loc_count = loc_tiles.shape[1]
    pairs = nblock * loc_count
    q = lax.axis_index("mem").astype(jnp.int32)
    q1 = q.reshape(1)
    order = jnp.stack([q, q ^ 1, 3 - q, q ^ 2])
    tile = lax.axis_index("tile").astype(jnp.int32)
    place = jnp.stack([tile // (DEPTH * CORES), (tile // CORES) & (DEPTH - 1), tile & (CORES - 1)])

    gain, innov, m1, m2, m3 = first_parts(
        q1, obs_anom, inverses, innovations, precision, obs_count
    )
    m1, m2, m3 = shift(m1, 1), shift(m2, 2), shift(m3, 3)

    tiles = columns * DEPTH * CORES
    loc = loc_tiles.reshape(pairs, 1)
    hits = (loc == lax.broadcasted_iota(jnp.int32, (pairs, tiles), 1)).astype(jnp.float32)
    same_tile = (loc == loc_tiles.reshape(1, pairs)).astype(jnp.float32)
    pair_at = lax.broadcasted_iota(jnp.int32, (pairs, 1), 0)
    earlier = (lax.broadcasted_iota(jnp.int32, (pairs, pairs), 1) < pair_at).astype(jnp.float32)
    rank = jnp.sum(same_tile * earlier, axis=1, keepdims=True)
    ranked = jnp.concatenate([hits * (rank == r).astype(jnp.float32) for r in range(SLOTS)], axis=1)
    block_of = (pair_at // loc_count).astype(jnp.float32)
    chosen = jnp.sum(ranked * block_of, axis=0, keepdims=True)
    tapers = jnp.sum(ranked * taper_weight.reshape(pairs, 1), axis=0, keepdims=True)

    half = rows // 2
    chosen, tapers, m1, m2, m3, low, high = lax.optimization_barrier(
        (chosen, tapers, m1, m2, m3, ensemble[:half], ensemble[half:])
    )
    a2, b1 = swap_a(high), swap_b(low)
    a1, b2 = swap_a(low), swap_b(high)

    up, down = (0, 1, 0), (0, -1, 0)
    own_blocks = tuple(merge(q1, chosen, tapers, (gain, innov, m1, m2, m3)))
    ups, downs = [own_blocks], [own_blocks]
    for _ in range(3):
        ups.append(tuple(move(x, columns, up) for x in ups[-1]))
        downs.append(tuple(move(x, columns, down) for x in downs[-1]))
    token = arrived(a2, b1)
    token, far = lax.optimization_barrier((token, (ups[-1][0], downs[-1][1])))
    far = (move(far[0], columns, up), move(far[1], columns, down))
    held = ups + downs[1:] + [far]
    lows, highs = [h[0] for h in held], [h[1] for h in held]
    others = sums(0, token, place, lows, highs)
    others = [move(x, columns, (0, 0, 1)) for x in others]
    here, e1, e2, e3 = sums(1, token, place, lows, highs, others)
    here, a1, b2 = lax.optimization_barrier((here, a1, b2))
    o1, o2 = swap_b(a1), swap_a(b2)
    e1, e2, e3 = move(e1, columns, (1, 0, 0)), move(e2, columns, (2, 0, 0)), move(e3, columns, (3, 0, 0))
    t0, t1, t2, t3 = transform_parts(q1, token, (here, e1, e2, e3))
    pieces = [t0, shift(t1, 1), shift(t2, 2), shift(t3, 3)]
    held = hold(ensemble, (a1, a2, b1, b2))
    return update(order, pieces, held, (o1, o2))


def solution(mesh):
    return jax.shard_map(
        per_device,
        mesh=mesh,
        in_specs=(
            P("tile", "mem"),
            P("tile", None, "mem"),
            P("tile", None, "mem"),
            P("tile", None, "mem"),
            P("tile", None),
            P("tile"),
            P("tile", None),
            P("tile", None),
        ),
        out_specs=P("tile", "mem"),
        check_vma=False,
    )
```

```python
import functools
import math

import jax
import jax.numpy as jnp
from jax import lax
from jax.experimental import pallas as pl
from jax.experimental.pallas import tpu as pltpu
from jax.sharding import PartitionSpec as P

VMEM_LIMIT = 24 * 1024 * 1024
FIRST_LIMIT = 60 * 1024 * 1024
GROUPS = 4
DEPTH = 8
CORES = 2
SLOTS = 2
STEPS = 4
SMALL = pl.CostEstimate(flops=10**6, bytes_accessed=10**6, transcendentals=0)


def first_kernel(
    q_ref, obs_ref, inv_ref, innov_ref, precision_ref, count_ref,
    gain_ref, innov_out_ref, m1_ref, m2_ref, m3_ref, rows_ref, live_ref,
):
    quarter, members = gain_ref.shape[1:]
    obs_rows, part = innov_ref.shape[1:]
    blocks = obs_ref.shape[0]
    q = q_ref[0]
    step = pl.program_id(0)
    position = lax.broadcasted_iota(jnp.int32, (obs_rows, part), 0)
    for k in range(blocks):
        rows_ref[...] = lax.dot_general(
            obs_ref[k], inv_ref[k], (((1,), (1,)), ((), ())), preferred_element_type=jnp.float32
        )
        block = step * blocks + k
        scale = jnp.broadcast_to(precision_ref[pl.ds(block, 1), :], (part, obs_rows)).T
        live_ref[...] = jnp.where(
            position < count_ref[block], scale * innov_ref[k].astype(jnp.float32), 0.0
        )
        own = pl.ds(pl.multiple_of(q * quarter, quarter), quarter)
        gain_ref[k] = rows_ref[own, :]
        innov_out_ref[k] = live_ref[own, :].astype(jnp.bfloat16)
        for d, ref in ((1, m1_ref), (2, m2_ref), (3, m3_ref)):
            rows = pl.ds(pl.multiple_of(lax.rem(q + d, GROUPS) * quarter, quarter), quarter)
            ref[k, :, :members] = rows_ref[rows, :].astype(jnp.bfloat16)
            ref[k, :, members:] = live_ref[rows, :].astype(jnp.bfloat16)


def first_parts(q, obs_anom, inverses, innovations, precision, obs_count):
    nblock, obs_rows, part = obs_anom.shape
    members = inverses.shape[1]
    quarter = obs_rows // GROUPS
    step = 8
    widths = [members, part] + [members + part] * 3
    types = [jnp.float32] + [jnp.bfloat16] * 4
    rows = pl.BlockSpec((step, obs_rows, part), lambda i, q: (i, 0, 0))
    return pl.pallas_call(
        first_kernel,
        grid_spec=pltpu.PrefetchScalarGridSpec(
            num_scalar_prefetch=1,
            grid=(nblock // step,),
            in_specs=[
                rows,
                pl.BlockSpec((step, members, part), lambda i, q: (i, 0, 0)),
                rows,
                pl.BlockSpec((nblock, obs_rows), lambda i, q: (0, 0)),
                pl.BlockSpec(memory_space=pltpu.SMEM),
            ],
            out_specs=[
                pl.BlockSpec((step, quarter, width), lambda i, q: (i, 0, 0)) for width in widths
            ],
            scratch_shapes=[
                pltpu.VMEM((obs_rows, members), jnp.float32),
                pltpu.VMEM((obs_rows, part), jnp.float32),
            ],
        ),
        out_shape=[
            jax.ShapeDtypeStruct((nblock, quarter, width), kind)
            for width, kind in zip(widths, types)
        ],
        compiler_params=pltpu.CompilerParams(vmem_limit_bytes=FIRST_LIMIT),
    )(q, obs_anom, inverses, innovations, precision, obs_count)


def merge_kernel(
    q_ref, early_ref, chosen_ref, taper_ref, gain_ref, innov_ref, r1_ref, r2_ref, r3_ref, low_ref, high_ref
):
    members = gain_ref.shape[2]
    part = innov_ref.shape[2]
    half = high_ref.shape[0]
    q = q_ref[0]
    gain = (
        gain_ref[...]
        + r1_ref[:, :, :members].astype(jnp.float32)
        + r2_ref[:, :, :members].astype(jnp.float32)
        + r3_ref[:, :, :members].astype(jnp.float32)
    ).astype(jnp.bfloat16)
    for out_ref, blocks in ((low_ref, slice(0, half)), (high_ref, slice(half, 2 * half))):
        out_ref[:half, :, :members] = gain[blocks]
        start = pl.multiple_of(members + q * part, part)
        out_ref[:half, :, pl.ds(start, part)] = innov_ref[blocks]
        for d, ref in ((1, r1_ref), (2, r2_ref), (3, r3_ref)):
            start = pl.multiple_of(members + lax.rem(q - d + GROUPS, GROUPS) * part, part)
            out_ref[:half, :, pl.ds(start, part)] = ref[blocks, :, members:]
    lanes = chosen_ref.shape[1]
    low_ref[half] = jnp.zeros(low_ref.shape[1:], low_ref.dtype)
    quarter = low_ref.shape[1]
    rest = jnp.broadcast_to(taper_ref[...], (quarter, lanes))
    low_ref[half, :, :lanes] = jnp.broadcast_to(chosen_ref[...], (quarter, lanes)).astype(jnp.bfloat16)
    for k in range(1, 4):
        term = rest.astype(jnp.bfloat16)
        rest = rest - term.astype(jnp.float32)
        low_ref[half, :, k * lanes : (k + 1) * lanes] = term


def merge(q, early, chosen, taper, parts):
    nblock, quarter, members = parts[0].shape
    half = nblock // 2
    vmem = pl.BlockSpec(memory_space=pltpu.VMEM)
    return pl.pallas_call(
        merge_kernel,
        in_specs=[pl.BlockSpec(memory_space=pltpu.SMEM)] * 2 + [vmem] * (2 + len(parts)),
        out_specs=[vmem] * 2,
        out_shape=[
            jax.ShapeDtypeStruct((half + 1, quarter, 2 * members), jnp.bfloat16),
            jax.ShapeDtypeStruct((half, quarter, 2 * members), jnp.bfloat16),
        ],
        compiler_params=pltpu.CompilerParams(vmem_limit_bytes=VMEM_LIMIT),
        cost_estimate=SMALL,
    )(q, early, chosen, taper, *parts)


def sums_kernel(same, token_ref, place_ref, *refs):
    lows, highs, refs = refs[:DEPTH], refs[DEPTH : 2 * DEPTH], refs[2 * DEPTH :]
    others, outs = (), ()
    if same:
        others, outs, refs = refs[:CORES], refs[CORES : CORES + GROUPS], refs[CORES + GROUPS :]
    else:
        outs, refs = refs[:CORES], refs[CORES:]
    pack = GROUPS // CORES
    all_ref, gain_ref, innov_ref, chosen_ref, taper_ref, chosen_smem, taper_smem, sems = refs
    half, quarter, width = highs[0].shape
    members = width // 2
    lanes = chosen_ref.shape[1]
    copies = []
    for k in range(DEPTH):
        copies.append(pltpu.make_async_copy(lows[k], all_ref.at[k, pl.ds(0, half + 1)], sems.at[2 * k]))
        copies.append(
            pltpu.make_async_copy(highs[k], all_ref.at[k, pl.ds(half + 1, half)], sems.at[2 * k + 1])
        )
    for copy in copies:
        copy.start()
    for k in range(DEPTH):
        copies[2 * k].wait()
        meta = all_ref[k, half, :, : 4 * lanes].astype(jnp.float32)[0:1]
        block = meta[:, :lanes].astype(jnp.int32)
        chosen_ref[pl.ds(k, 1), :] = block + jnp.where(block < half, 0, 1)
        taper_ref[pl.ds(k, 1), :] = (
            meta[:, lanes : 2 * lanes] + meta[:, 2 * lanes : 3 * lanes] + meta[:, 3 * lanes :]
        )
    tables = [
        pltpu.make_async_copy(chosen_ref, chosen_smem, sems.at[2 * DEPTH]),
        pltpu.make_async_copy(taper_ref, taper_smem, sems.at[2 * DEPTH + 1]),
    ]
    for copy in tables:
        copy.start()
    for k in range(DEPTH):
        copies[2 * k + 1].wait()
    for copy in tables:
        copy.wait()
    core = place_ref[2] if same else 1 - place_ref[2]
    for away in range(GROUPS):
        column = lax.rem(place_ref[0] + away, GROUPS)
        tile = (column * DEPTH + place_ref[1]) * CORES + core
        for k in range(DEPTH):
            for r in range(SLOTS):
                entry = r * (lanes // SLOTS) + tile
                block = chosen_smem[k, entry]
                rows = pl.ds((k * SLOTS + r) * quarter, quarter)
                gain = all_ref[k, block, :, :members].astype(jnp.float32)
                gain_ref[away, rows, :] = (taper_smem[k, entry] * gain).astype(jnp.bfloat16)
                innov_ref[away, rows, :] = all_ref[k, block, :, members:]
        total = lax.dot_general(
            gain_ref[away],
            innov_ref[away],
            (((0,), (0,)), ((), ())),
            preferred_element_type=jnp.float32,
        )
        if same:
            total = total + others[away // pack][away % pack].astype(jnp.float32)
            outs[away][...] = total.astype(outs[away].dtype)
        else:
            outs[away // pack][away % pack] = total.astype(jnp.bfloat16)


def sums(same, token, place, lows, highs, others=()):
    half, quarter, width = highs[0].shape
    members = width // 2
    lanes = 128
    square = (members, members)
    if same:
        kinds = [jnp.float32] + [jnp.bfloat16] * (GROUPS - 1)
        out_shape = [jax.ShapeDtypeStruct(square, kind) for kind in kinds]
    else:
        shape = (GROUPS // CORES,) + square
        out_shape = [jax.ShapeDtypeStruct(shape, jnp.bfloat16)] * CORES
    taken = (GROUPS, DEPTH * SLOTS * quarter, members)
    return pl.pallas_call(
        functools.partial(sums_kernel, same),
        in_specs=[pl.BlockSpec(memory_space=pltpu.SMEM)] * 2
        + [pl.BlockSpec(memory_space=pl.ANY)] * (2 * DEPTH)
        + [pl.BlockSpec(memory_space=pltpu.VMEM)] * len(others),
        out_specs=[pl.BlockSpec(memory_space=pltpu.VMEM)] * len(out_shape),
        out_shape=out_shape,
        scratch_shapes=[
            pltpu.VMEM((DEPTH, 2 * half + 1, quarter, width), jnp.bfloat16),
            pltpu.VMEM(taken, jnp.bfloat16),
            pltpu.VMEM(taken, jnp.bfloat16),
            pltpu.VMEM((DEPTH, lanes), jnp.int32),
            pltpu.VMEM((DEPTH, lanes), jnp.float32),
            pltpu.SMEM((DEPTH, lanes), jnp.int32),
            pltpu.SMEM((DEPTH, lanes), jnp.float32),
            pltpu.SemaphoreType.DMA((2 * DEPTH + 2,)),
        ],
        compiler_params=pltpu.CompilerParams(vmem_limit_bytes=VMEM_LIMIT),
        cost_estimate=SMALL,
    )(token, place, *lows, *highs, *others)


def arrived_kernel(*refs):
    refs[-1][0] = 0


def arrived(*arrays):
    return pl.pallas_call(
        arrived_kernel,
        in_specs=[pl.BlockSpec(memory_space=pl.ANY)] * len(arrays),
        out_specs=pl.BlockSpec(memory_space=pltpu.SMEM),
        out_shape=jax.ShapeDtypeStruct((1,), jnp.int32),
        cost_estimate=pl.CostEstimate(flops=10**12, bytes_accessed=10**9, transcendentals=0),
    )(*arrays)


def transform_kernel(q_ref, token_ref, r0_ref, r1_ref, r2_ref, r3_ref, own_ref, s1_ref, s2_ref, s3_ref):
    q = q_ref[0]
    members, part = own_ref.shape
    for d, out_ref in enumerate((own_ref, s1_ref, s2_ref, s3_ref)):
        columns = pl.ds(pl.multiple_of(lax.rem(q + d, GROUPS) * part, part), part)
        total = (
            r0_ref[:, columns]
            + r1_ref[:, columns].astype(jnp.float32)
            + r2_ref[:, columns].astype(jnp.float32)
            + r3_ref[:, columns].astype(jnp.float32)
        )
        mean = jnp.sum(total, axis=0, keepdims=True) / members
        out_ref[...] = ((total - mean) * (1.0 / math.sqrt(members - 1))).astype(out_ref.dtype)


def transform_parts(q, token, sums_here):
    members = sums_here[0].shape[0]
    part = members // GROUPS
    return pl.pallas_call(
        transform_kernel,
        in_specs=[pl.BlockSpec(memory_space=pltpu.SMEM)] * 2
        + [pl.BlockSpec(memory_space=pltpu.VMEM)] * GROUPS,
        out_specs=[pl.BlockSpec(memory_space=pltpu.VMEM)] * GROUPS,
        out_shape=[jax.ShapeDtypeStruct((members, part), jnp.float32)]
        + [jax.ShapeDtypeStruct((members, part), jnp.bfloat16)] * 3,
        compiler_params=pltpu.CompilerParams(vmem_limit_bytes=VMEM_LIMIT),
        cost_estimate=pl.CostEstimate(flops=5*10**9, bytes_accessed=10**6, transcendentals=0),
    )(q, token, *sums_here)


def hold_kernel(own_ref, a1_ref, a2_ref, b1_ref, b2_ref, out_ref, sems):
    half = a1_ref.shape[0]
    copies = [pltpu.make_async_copy(own_ref, out_ref.at[0], sems.at[0])]
    for k, (low, high) in enumerate(((a1_ref, a2_ref), (b1_ref, b2_ref))):
        copies.append(
            pltpu.make_async_copy(low, out_ref.at[k + 1, pl.ds(0, half)], sems.at[2 * k + 1])
        )
        copies.append(
            pltpu.make_async_copy(high, out_ref.at[k + 1, pl.ds(half, half)], sems.at[2 * k + 2])
        )
    for copy in copies:
        copy.start()
    for copy in copies:
        copy.wait()


def hold(own, others):
    rows, part = own.shape
    return pl.pallas_call(
        hold_kernel,
        in_specs=[pl.BlockSpec(memory_space=pl.ANY)] * (1 + len(others)),
        out_specs=pl.BlockSpec(memory_space=pltpu.VMEM),
        out_shape=jax.ShapeDtypeStruct((GROUPS - 1, rows, part), jnp.bfloat16),
        scratch_shapes=[pltpu.SemaphoreType.DMA((5,))],
        compiler_params=pltpu.CompilerParams(vmem_limit_bytes=16 * 1024 * 1024),
        cost_estimate=SMALL,
    )(own, *others)


def update_kernel(
    order_ref, t0_ref, t1_ref, t2_ref, t3_ref, held_ref, o1_ref, o2_ref,
    out_ref, raw_ref, weights_ref, far_ref, result_ref, in_sems, out_sems,
):
    part = held_ref.shape[2]
    step = result_ref.shape[1]
    half = STEPS // 2
    loads = []
    for i in range(STEPS):
        ref = o1_ref if i < half else o2_ref
        loads.append(
            pltpu.make_async_copy(ref.at[pl.ds((i % half) * step, step)], far_ref.at[i], in_sems.at[i])
        )
        loads[-1].start()
    total = (
        t0_ref[...]
        + t1_ref[...].astype(jnp.float32)
        + t2_ref[...].astype(jnp.float32)
        + t3_ref[...].astype(jnp.float32)
    ).astype(jnp.bfloat16)
    raw_ref[...] = total.reshape(raw_ref.shape)
    for k in range(GROUPS):
        weights_ref[pl.ds(k * part, part), :] = raw_ref[order_ref[k]]
    stores = []
    for i in range(STEPS):
        loads[i].wait()
        rows = pl.ds(i * step, step)
        near = [held_ref[k, rows, :] for k in range(GROUPS - 1)]
        states = jnp.concatenate(near + [far_ref[i]], axis=1)
        increment = jnp.dot(states, weights_ref[...], preferred_element_type=jnp.float32)
        result_ref[i] = (near[0].astype(jnp.float32) + increment).astype(result_ref.dtype)
        stores.append(pltpu.make_async_copy(result_ref.at[i], out_ref.at[rows], out_sems.at[i]))
        stores[-1].start()
    for store in stores:
        store.wait()


def update(order, pieces, held, others):
    rows, part = held.shape[1:]
    members = pieces[0].shape[0]
    step = rows // STEPS
    return pl.pallas_call(
        update_kernel,
        in_specs=[pl.BlockSpec(memory_space=pltpu.SMEM)]
        + [pl.BlockSpec(memory_space=pltpu.VMEM)] * (GROUPS + 1)
        + [pl.BlockSpec(memory_space=pl.ANY)] * len(others),
        out_specs=pl.BlockSpec(memory_space=pl.ANY),
        out_shape=jax.ShapeDtypeStruct((rows, part), jnp.bfloat16),
        scratch_shapes=[
            pltpu.VMEM((GROUPS, part, part), jnp.bfloat16),
            pltpu.VMEM((members, part), jnp.bfloat16),
            pltpu.VMEM((STEPS, step, part), jnp.bfloat16),
            pltpu.VMEM((STEPS, step, part), jnp.bfloat16),
            pltpu.SemaphoreType.DMA((STEPS,)),
            pltpu.SemaphoreType.DMA((STEPS,)),
        ],
        compiler_params=pltpu.CompilerParams(vmem_limit_bytes=VMEM_LIMIT),
    )(order, *pieces, held, *others)


def shift(x, d):
    return lax.ppermute(x, "mem", [(i, (i + d) % GROUPS) for i in range(GROUPS)])


def swap_a(x):
    return lax.ppermute(x, "mem", [(0, 1), (1, 0), (2, 3), (3, 2)])


def swap_b(x):
    return lax.ppermute(x, "mem", [(0, 3), (3, 0), (1, 2), (2, 1)])


def move(x, columns, away=(0, 0, 0)):
    pairs = []
    for c in range(columns):
        for z in range(DEPTH):
            for k in range(CORES):
                target = (c + away[0]) % columns, (z + away[1]) % DEPTH, (k + away[2]) % CORES
                pairs.append(
                    ((c * DEPTH + z) * CORES + k, (target[0] * DEPTH + target[1]) * CORES + target[2])
                )
    return lax.ppermute(x, "tile", pairs)


def per_device(
    ensemble, obs_anom, inverses, innovations, precision, obs_count, loc_tiles, taper_weight
):
    columns = lax.axis_size("tile") // (DEPTH * CORES)
    nblock = obs_anom.shape[0]
    rows = ensemble.shape[0]
    loc_count = loc_tiles.shape[1]
    pairs = nblock * loc_count
    q = lax.axis_index("mem").astype(jnp.int32)
    q1 = q.reshape(1)
    order = jnp.stack([q, q ^ 1, 3 - q, q ^ 2])
    tile = lax.axis_index("tile").astype(jnp.int32)
    place = jnp.stack([tile // (DEPTH * CORES), (tile // CORES) & (DEPTH - 1), tile & (CORES - 1)])

    gain, innov, m1, m2, m3 = first_parts(
        q1, obs_anom, inverses, innovations, precision, obs_count
    )
    m1, m2, m3 = shift(m1, 1), shift(m2, 2), shift(m3, 3)

    tiles = columns * DEPTH * CORES
    loc = loc_tiles.reshape(pairs, 1)
    hits = (loc == lax.broadcasted_iota(jnp.int32, (pairs, tiles), 1)).astype(jnp.float32)
    same_tile = (loc == loc_tiles.reshape(1, pairs)).astype(jnp.float32)
    pair_at = lax.broadcasted_iota(jnp.int32, (pairs, 1), 0)
    earlier = (lax.broadcasted_iota(jnp.int32, (pairs, pairs), 1) < pair_at).astype(jnp.float32)
    rank = jnp.sum(same_tile * earlier, axis=1, keepdims=True)
    ranked = jnp.concatenate([hits * (rank == r).astype(jnp.float32) for r in range(SLOTS)], axis=1)
    block_of = (pair_at // loc_count).astype(jnp.float32)
    chosen = jnp.sum(ranked * block_of, axis=0, keepdims=True)
    tapers = jnp.sum(ranked * taper_weight.reshape(pairs, 1), axis=0, keepdims=True)

    half = rows // 2
    early = arrived(m1, m3)
    m1, m3, low, high = lax.optimization_barrier((m1, m3, ensemble[:half], ensemble[half:]))
    a2, b1 = swap_a(high), swap_b(low)
    a1, b2 = swap_a(low), swap_b(high)

    up, down = (0, 1, 0), (0, -1, 0)
    own_blocks = tuple(merge(q1, early, chosen, tapers, (gain, innov, m1, m2, m3)))
    ups, downs = [own_blocks], [own_blocks]
    for _ in range(3):
        ups.append(tuple(move(x, columns, up) for x in ups[-1]))
        downs.append(tuple(move(x, columns, down) for x in downs[-1]))
    token = arrived(a2, b1)
    token, far = lax.optimization_barrier((token, (ups[-1][0], downs[-1][1])))
    far = (move(far[0], columns, up), move(far[1], columns, down))
    held = ups + downs[1:] + [far]
    lows, highs = [h[0] for h in held], [h[1] for h in held]
    others = sums(0, token, place, lows, highs)
    others = [move(x, columns, (0, 0, 1)) for x in others]
    here, e1, e2, e3 = sums(1, token, place, lows, highs, others)
    here, a1, b2 = lax.optimization_barrier((here, a1, b2))
    o1, o2 = swap_b(a1), swap_a(b2)
    e1, e2, e3 = move(e1, columns, (1, 0, 0)), move(e2, columns, (2, 0, 0)), move(e3, columns, (3, 0, 0))
    t0, t1, t2, t3 = transform_parts(q1, token, (here, e1, e2, e3))
    pieces = [t0, shift(t1, 1), shift(t2, 2), shift(t3, 3)]
    held = hold(ensemble, (a1, a2, b1, b2))
    return update(order, pieces, held, (o1, o2))


def solution(mesh):
    return jax.shard_map(
        per_device,
        mesh=mesh,
        in_specs=(
            P("tile", "mem"),
            P("tile", None, "mem"),
            P("tile", None, "mem"),
            P("tile", None, "mem"),
            P("tile", None),
            P("tile"),
            P("tile", None),
            P("tile", None),
        ),
        out_specs=P("tile", "mem"),
        check_vma=False,
    )
```

```python
import functools
import math

import jax
import jax.numpy as jnp
from jax import lax
from jax.experimental import pallas as pl
from jax.experimental.pallas import tpu as pltpu
from jax.sharding import PartitionSpec as P

VMEM_LIMIT = 24 * 1024 * 1024
FIRST_LIMIT = 60 * 1024 * 1024
GROUPS = 4
DEPTH = 8
CORES = 2
SLOTS = 2
STEPS = 4
SMALL = pl.CostEstimate(flops=10**6, bytes_accessed=10**6, transcendentals=0)


def first_kernel(
    q_ref, obs_ref, inv_ref, innov_ref, precision_ref, count_ref,
    gain_ref, innov_out_ref, m1_ref, m2_ref, m3_ref, rows_ref, live_ref,
):
    quarter, members = gain_ref.shape[1:]
    obs_rows, part = innov_ref.shape[1:]
    blocks = obs_ref.shape[0]
    q = q_ref[0]
    step = pl.program_id(0)
    position = lax.broadcasted_iota(jnp.int32, (obs_rows, part), 0)
    for k in range(blocks):
        rows_ref[...] = lax.dot_general(
            obs_ref[k], inv_ref[k], (((1,), (1,)), ((), ())), preferred_element_type=jnp.float32
        )
        block = step * blocks + k
        scale = jnp.broadcast_to(precision_ref[pl.ds(block, 1), :], (part, obs_rows)).T
        live_ref[...] = jnp.where(
            position < count_ref[block], scale * innov_ref[k].astype(jnp.float32), 0.0
        )
        own = pl.ds(pl.multiple_of(q * quarter, quarter), quarter)
        gain_ref[k] = rows_ref[own, :]
        innov_out_ref[k] = live_ref[own, :].astype(jnp.bfloat16)
        for d, ref in ((1, m1_ref), (2, m2_ref), (3, m3_ref)):
            rows = pl.ds(pl.multiple_of(lax.rem(q + d, GROUPS) * quarter, quarter), quarter)
            ref[k, :, :members] = rows_ref[rows, :].astype(jnp.bfloat16)
            ref[k, :, members:] = live_ref[rows, :].astype(jnp.bfloat16)


def first_parts(q, obs_anom, inverses, innovations, precision, obs_count):
    nblock, obs_rows, part = obs_anom.shape
    members = inverses.shape[1]
    quarter = obs_rows // GROUPS
    step = 8
    widths = [members, part] + [members + part] * 3
    types = [jnp.float32] + [jnp.bfloat16] * 4
    rows = pl.BlockSpec((step, obs_rows, part), lambda i, q: (i, 0, 0))
    return pl.pallas_call(
        first_kernel,
        grid_spec=pltpu.PrefetchScalarGridSpec(
            num_scalar_prefetch=1,
            grid=(nblock // step,),
            in_specs=[
                rows,
                pl.BlockSpec((step, members, part), lambda i, q: (i, 0, 0)),
                rows,
                pl.BlockSpec((nblock, obs_rows), lambda i, q: (0, 0)),
                pl.BlockSpec(memory_space=pltpu.SMEM),
            ],
            out_specs=[
                pl.BlockSpec((step, quarter, width), lambda i, q: (i, 0, 0)) for width in widths
            ],
            scratch_shapes=[
                pltpu.VMEM((obs_rows, members), jnp.float32),
                pltpu.VMEM((obs_rows, part), jnp.float32),
            ],
        ),
        out_shape=[
            jax.ShapeDtypeStruct((nblock, quarter, width), kind)
            for width, kind in zip(widths, types)
        ],
        compiler_params=pltpu.CompilerParams(vmem_limit_bytes=FIRST_LIMIT),
    )(q, obs_anom, inverses, innovations, precision, obs_count)


def merge_kernel(
    q_ref, early_ref, chosen_ref, taper_ref, gain_ref, innov_ref, r1_ref, r2_ref, r3_ref, low_ref, high_ref
):
    members = gain_ref.shape[2]
    part = innov_ref.shape[2]
    half = high_ref.shape[0]
    q = q_ref[0]
    gain = (
        gain_ref[...]
        + r1_ref[:, :, :members].astype(jnp.float32)
        + r2_ref[:, :, :members].astype(jnp.float32)
        + r3_ref[:, :, :members].astype(jnp.float32)
    ).astype(jnp.bfloat16)
    for out_ref, blocks in ((low_ref, slice(0, half)), (high_ref, slice(half, 2 * half))):
        out_ref[:half, :, :members] = gain[blocks]
        start = pl.multiple_of(members + q * part, part)
        out_ref[:half, :, pl.ds(start, part)] = innov_ref[blocks]
        for d, ref in ((1, r1_ref), (2, r2_ref), (3, r3_ref)):
            start = pl.multiple_of(members + lax.rem(q - d + GROUPS, GROUPS) * part, part)
            out_ref[:half, :, pl.ds(start, part)] = ref[blocks, :, members:]
    lanes = chosen_ref.shape[1]
    low_ref[half] = jnp.zeros(low_ref.shape[1:], low_ref.dtype)
    quarter = low_ref.shape[1]
    rest = jnp.broadcast_to(taper_ref[...], (quarter, lanes))
    low_ref[half, :, :lanes] = jnp.broadcast_to(chosen_ref[...], (quarter, lanes)).astype(jnp.bfloat16)
    for k in range(1, 4):
        term = rest.astype(jnp.bfloat16)
        rest = rest - term.astype(jnp.float32)
        low_ref[half, :, k * lanes : (k + 1) * lanes] = term


def merge(q, early, chosen, taper, parts):
    nblock, quarter, members = parts[0].shape
    half = nblock // 2
    vmem = pl.BlockSpec(memory_space=pltpu.VMEM)
    return pl.pallas_call(
        merge_kernel,
        in_specs=[pl.BlockSpec(memory_space=pltpu.SMEM)] * 2 + [vmem] * (2 + len(parts)),
        out_specs=[vmem] * 2,
        out_shape=[
            jax.ShapeDtypeStruct((half + 1, quarter, 2 * members), jnp.bfloat16),
            jax.ShapeDtypeStruct((half, quarter, 2 * members), jnp.bfloat16),
        ],
        compiler_params=pltpu.CompilerParams(vmem_limit_bytes=VMEM_LIMIT),
        cost_estimate=SMALL,
    )(q, early, chosen, taper, *parts)


def sums_kernel(same, token_ref, place_ref, *refs):
    lows, highs, refs = refs[:DEPTH], refs[DEPTH : 2 * DEPTH], refs[2 * DEPTH :]
    others, outs = (), ()
    if same:
        others, outs, refs = refs[:CORES], refs[CORES : CORES + GROUPS], refs[CORES + GROUPS :]
    else:
        outs, refs = refs[:CORES], refs[CORES:]
    pack = GROUPS // CORES
    all_ref, gain_ref, innov_ref, chosen_ref, taper_ref, chosen_smem, taper_smem, sems = refs
    half, quarter, width = highs[0].shape
    members = width // 2
    lanes = chosen_ref.shape[1]
    copies = []
    for k in range(DEPTH):
        copies.append(pltpu.make_async_copy(lows[k], all_ref.at[k, pl.ds(0, half + 1)], sems.at[2 * k]))
        copies.append(
            pltpu.make_async_copy(highs[k], all_ref.at[k, pl.ds(half + 1, half)], sems.at[2 * k + 1])
        )
    for copy in copies:
        copy.start()
    for k in range(DEPTH):
        copies[2 * k].wait()
        meta = all_ref[k, half, :, : 4 * lanes].astype(jnp.float32)[0:1]
        block = meta[:, :lanes].astype(jnp.int32)
        chosen_ref[pl.ds(k, 1), :] = block + jnp.where(block < half, 0, 1)
        taper_ref[pl.ds(k, 1), :] = (
            meta[:, lanes : 2 * lanes] + meta[:, 2 * lanes : 3 * lanes] + meta[:, 3 * lanes :]
        )
    tables = [
        pltpu.make_async_copy(chosen_ref, chosen_smem, sems.at[2 * DEPTH]),
        pltpu.make_async_copy(taper_ref, taper_smem, sems.at[2 * DEPTH + 1]),
    ]
    for copy in tables:
        copy.start()
    for k in range(DEPTH):
        copies[2 * k + 1].wait()
    for copy in tables:
        copy.wait()
    core = place_ref[2] if same else 1 - place_ref[2]
    for away in range(GROUPS):
        column = lax.rem(place_ref[0] + away, GROUPS)
        tile = (column * DEPTH + place_ref[1]) * CORES + core
        for k in range(DEPTH):
            for r in range(SLOTS):
                entry = r * (lanes // SLOTS) + tile
                block = chosen_smem[k, entry]
                rows = pl.ds((k * SLOTS + r) * quarter, quarter)
                gain = all_ref[k, block, :, :members].astype(jnp.float32)
                gain_ref[away, rows, :] = (taper_smem[k, entry] * gain).astype(jnp.bfloat16)
                innov_ref[away, rows, :] = all_ref[k, block, :, members:]
        total = lax.dot_general(
            gain_ref[away],
            innov_ref[away],
            (((0,), (0,)), ((), ())),
            preferred_element_type=jnp.float32,
        )
        if same:
            total = total + others[away // pack][away % pack].astype(jnp.float32)
            outs[away][...] = total.astype(outs[away].dtype)
        else:
            outs[away // pack][away % pack] = total.astype(jnp.bfloat16)


def sums(same, token, place, lows, highs, others=()):
    half, quarter, width = highs[0].shape
    members = width // 2
    lanes = 128
    square = (members, members)
    if same:
        kinds = [jnp.float32] + [jnp.bfloat16] * (GROUPS - 1)
        out_shape = [jax.ShapeDtypeStruct(square, kind) for kind in kinds]
    else:
        shape = (GROUPS // CORES,) + square
        out_shape = [jax.ShapeDtypeStruct(shape, jnp.bfloat16)] * CORES
    taken = (GROUPS, DEPTH * SLOTS * quarter, members)
    return pl.pallas_call(
        functools.partial(sums_kernel, same),
        in_specs=[pl.BlockSpec(memory_space=pltpu.SMEM)] * 2
        + [pl.BlockSpec(memory_space=pl.ANY)] * (2 * DEPTH)
        + [pl.BlockSpec(memory_space=pltpu.VMEM)] * len(others),
        out_specs=[pl.BlockSpec(memory_space=pltpu.VMEM)] * len(out_shape),
        out_shape=out_shape,
        scratch_shapes=[
            pltpu.VMEM((DEPTH, 2 * half + 1, quarter, width), jnp.bfloat16),
            pltpu.VMEM(taken, jnp.bfloat16),
            pltpu.VMEM(taken, jnp.bfloat16),
            pltpu.VMEM((DEPTH, lanes), jnp.int32),
            pltpu.VMEM((DEPTH, lanes), jnp.float32),
            pltpu.SMEM((DEPTH, lanes), jnp.int32),
            pltpu.SMEM((DEPTH, lanes), jnp.float32),
            pltpu.SemaphoreType.DMA((2 * DEPTH + 2,)),
        ],
        compiler_params=pltpu.CompilerParams(vmem_limit_bytes=VMEM_LIMIT),
        cost_estimate=SMALL,
    )(token, place, *lows, *highs, *others)


def arrived_kernel(*refs):
    refs[-1][0] = 0


def arrived(*arrays):
    return pl.pallas_call(
        arrived_kernel,
        in_specs=[pl.BlockSpec(memory_space=pl.ANY)] * len(arrays),
        out_specs=pl.BlockSpec(memory_space=pltpu.SMEM),
        out_shape=jax.ShapeDtypeStruct((1,), jnp.int32),
        cost_estimate=pl.CostEstimate(flops=10**12, bytes_accessed=10**9, transcendentals=0),
    )(*arrays)


def transform_kernel(q_ref, token_ref, r0_ref, r1_ref, r2_ref, r3_ref, own_ref, s1_ref, s2_ref, s3_ref):
    q = q_ref[0]
    members, part = own_ref.shape
    for d, out_ref in enumerate((own_ref, s1_ref, s2_ref, s3_ref)):
        columns = pl.ds(pl.multiple_of(lax.rem(q + d, GROUPS) * part, part), part)
        total = (
            r0_ref[:, columns]
            + r1_ref[:, columns].astype(jnp.float32)
            + r2_ref[:, columns].astype(jnp.float32)
            + r3_ref[:, columns].astype(jnp.float32)
        )
        mean = jnp.sum(total, axis=0, keepdims=True) / members
        out_ref[...] = ((total - mean) * (1.0 / math.sqrt(members - 1))).astype(out_ref.dtype)


def transform_parts(q, token, sums_here):
    members = sums_here[0].shape[0]
    part = members // GROUPS
    return pl.pallas_call(
        transform_kernel,
        in_specs=[pl.BlockSpec(memory_space=pltpu.SMEM)] * 2
        + [pl.BlockSpec(memory_space=pltpu.VMEM)] * GROUPS,
        out_specs=[pl.BlockSpec(memory_space=pltpu.VMEM)] * GROUPS,
        out_shape=[jax.ShapeDtypeStruct((members, part), jnp.float32)]
        + [jax.ShapeDtypeStruct((members, part), jnp.bfloat16)] * 3,
        compiler_params=pltpu.CompilerParams(vmem_limit_bytes=VMEM_LIMIT),
        cost_estimate=pl.CostEstimate(flops=5*10**9, bytes_accessed=10**6, transcendentals=0),
    )(q, token, *sums_here)


def hold_kernel(own_ref, a1_ref, a2_ref, b1_ref, b2_ref, out_ref, sems):
    half = a1_ref.shape[0]
    copies = [pltpu.make_async_copy(own_ref, out_ref.at[0], sems.at[0])]
    for k, (low, high) in enumerate(((a1_ref, a2_ref), (b1_ref, b2_ref))):
        copies.append(
            pltpu.make_async_copy(low, out_ref.at[k + 1, pl.ds(0, half)], sems.at[2 * k + 1])
        )
        copies.append(
            pltpu.make_async_copy(high, out_ref.at[k + 1, pl.ds(half, half)], sems.at[2 * k + 2])
        )
    for copy in copies:
        copy.start()
    for copy in copies:
        copy.wait()


def hold(own, others):
    rows, part = own.shape
    return pl.pallas_call(
        hold_kernel,
        in_specs=[pl.BlockSpec(memory_space=pl.ANY)] * (1 + len(others)),
        out_specs=pl.BlockSpec(memory_space=pltpu.VMEM),
        out_shape=jax.ShapeDtypeStruct((GROUPS - 1, rows, part), jnp.bfloat16),
        scratch_shapes=[pltpu.SemaphoreType.DMA((5,))],
        compiler_params=pltpu.CompilerParams(vmem_limit_bytes=16 * 1024 * 1024),
        cost_estimate=SMALL,
    )(own, *others)


def update_kernel(
    order_ref, t0_ref, t1_ref, t2_ref, t3_ref, held_ref, o1_ref, o2_ref,
    out_ref, raw_ref, weights_ref, far_ref, result_ref, in_sems, out_sems,
):
    part = held_ref.shape[2]
    step = result_ref.shape[1]
    half = STEPS // 2
    loads = []
    for i in range(STEPS):
        ref = o1_ref if i < half else o2_ref
        loads.append(
            pltpu.make_async_copy(ref.at[pl.ds((i % half) * step, step)], far_ref.at[i], in_sems.at[i])
        )
        loads[-1].start()
    total = (
        t0_ref[...]
        + t1_ref[...].astype(jnp.float32)
        + t2_ref[...].astype(jnp.float32)
        + t3_ref[...].astype(jnp.float32)
    ).astype(jnp.bfloat16)
    raw_ref[...] = total.reshape(raw_ref.shape)
    for k in range(GROUPS):
        weights_ref[pl.ds(k * part, part), :] = raw_ref[order_ref[k]]
    stores = []
    for i in range(STEPS):
        loads[i].wait()
        rows = pl.ds(i * step, step)
        near = [held_ref[k, rows, :] for k in range(GROUPS - 1)]
        states = jnp.concatenate(near + [far_ref[i]], axis=1)
        increment = jnp.dot(states, weights_ref[...], preferred_element_type=jnp.float32)
        result_ref[i] = (near[0].astype(jnp.float32) + increment).astype(result_ref.dtype)
        stores.append(pltpu.make_async_copy(result_ref.at[i], out_ref.at[rows], out_sems.at[i]))
        stores[-1].start()
    for store in stores:
        store.wait()


def update(order, pieces, held, others):
    rows, part = held.shape[1:]
    members = pieces[0].shape[0]
    step = rows // STEPS
    return pl.pallas_call(
        update_kernel,
        in_specs=[pl.BlockSpec(memory_space=pltpu.SMEM)]
        + [pl.BlockSpec(memory_space=pltpu.VMEM)] * (GROUPS + 1)
        + [pl.BlockSpec(memory_space=pl.ANY)] * len(others),
        out_specs=pl.BlockSpec(memory_space=pl.ANY),
        out_shape=jax.ShapeDtypeStruct((rows, part), jnp.bfloat16),
        scratch_shapes=[
            pltpu.VMEM((GROUPS, part, part), jnp.bfloat16),
            pltpu.VMEM((members, part), jnp.bfloat16),
            pltpu.VMEM((STEPS, step, part), jnp.bfloat16),
            pltpu.VMEM((STEPS, step, part), jnp.bfloat16),
            pltpu.SemaphoreType.DMA((STEPS,)),
            pltpu.SemaphoreType.DMA((STEPS,)),
        ],
        compiler_params=pltpu.CompilerParams(vmem_limit_bytes=VMEM_LIMIT),
    )(order, *pieces, held, *others)


def shift(x, d):
    return lax.ppermute(x, "mem", [(i, (i + d) % GROUPS) for i in range(GROUPS)])


def swap_a(x):
    return lax.ppermute(x, "mem", [(0, 1), (1, 0), (2, 3), (3, 2)])


def swap_b(x):
    return lax.ppermute(x, "mem", [(0, 3), (3, 0), (1, 2), (2, 1)])


def move(x, columns, away=(0, 0, 0)):
    pairs = []
    for c in range(columns):
        for z in range(DEPTH):
            for k in range(CORES):
                target = (c + away[0]) % columns, (z + away[1]) % DEPTH, (k + away[2]) % CORES
                pairs.append(
                    ((c * DEPTH + z) * CORES + k, (target[0] * DEPTH + target[1]) * CORES + target[2])
                )
    return lax.ppermute(x, "tile", pairs)


def per_device(
    ensemble, obs_anom, inverses, innovations, precision, obs_count, loc_tiles, taper_weight
):
    columns = lax.axis_size("tile") // (DEPTH * CORES)
    nblock = obs_anom.shape[0]
    rows = ensemble.shape[0]
    loc_count = loc_tiles.shape[1]
    pairs = nblock * loc_count
    q = lax.axis_index("mem").astype(jnp.int32)
    q1 = q.reshape(1)
    order = jnp.stack([q, q ^ 1, 3 - q, q ^ 2])
    tile = lax.axis_index("tile").astype(jnp.int32)
    place = jnp.stack([tile // (DEPTH * CORES), (tile // CORES) & (DEPTH - 1), tile & (CORES - 1)])

    gain, innov, m1, m2, m3 = first_parts(
        q1, obs_anom, inverses, innovations, precision, obs_count
    )
    m1, m2, m3 = shift(m1, 1), shift(m2, 2), shift(m3, 3)

    tiles = columns * DEPTH * CORES
    loc = loc_tiles.reshape(pairs, 1)
    hits = (loc == lax.broadcasted_iota(jnp.int32, (pairs, tiles), 1)).astype(jnp.float32)
    same_tile = (loc == loc_tiles.reshape(1, pairs)).astype(jnp.float32)
    pair_at = lax.broadcasted_iota(jnp.int32, (pairs, 1), 0)
    earlier = (lax.broadcasted_iota(jnp.int32, (pairs, pairs), 1) < pair_at).astype(jnp.float32)
    rank = jnp.sum(same_tile * earlier, axis=1, keepdims=True)
    ranked = jnp.concatenate([hits * (rank == r).astype(jnp.float32) for r in range(SLOTS)], axis=1)
    block_of = (pair_at // loc_count).astype(jnp.float32)
    chosen = jnp.sum(ranked * block_of, axis=0, keepdims=True)
    tapers = jnp.sum(ranked * taper_weight.reshape(pairs, 1), axis=0, keepdims=True)

    half = rows // 2
    early = arrived(m1, m3)
    m1, low, high = lax.optimization_barrier((m1, ensemble[:half], ensemble[half:]))
    a2, b1 = swap_a(high), swap_b(low)
    a1, b2 = swap_a(low), swap_b(high)

    up, down = (0, 1, 0), (0, -1, 0)
    own_blocks = tuple(merge(q1, early, chosen, tapers, (gain, innov, m1, m2, m3)))
    ups, downs = [own_blocks], [own_blocks]
    for _ in range(3):
        ups.append(tuple(move(x, columns, up) for x in ups[-1]))
        downs.append(tuple(move(x, columns, down) for x in downs[-1]))
    token = arrived(a2, b1)
    token, far = lax.optimization_barrier((token, (ups[-1][0], downs[-1][1])))
    far = (move(far[0], columns, up), move(far[1], columns, down))
    held = ups + downs[1:] + [far]
    lows, highs = [h[0] for h in held], [h[1] for h in held]
    others = sums(0, token, place, lows, highs)
    others = [move(x, columns, (0, 0, 1)) for x in others]
    here, e1, e2, e3 = sums(1, token, place, lows, highs, others)
    here, a1, b2 = lax.optimization_barrier((here, a1, b2))
    o1, o2 = swap_b(a1), swap_a(b2)
    e1, e2, e3 = move(e1, columns, (1, 0, 0)), move(e2, columns, (2, 0, 0)), move(e3, columns, (3, 0, 0))
    t0, t1, t2, t3 = transform_parts(q1, token, (here, e1, e2, e3))
    pieces = [t0, shift(t1, 1), shift(t2, 2), shift(t3, 3)]
    held = hold(ensemble, (a1, a2, b1, b2))
    return update(order, pieces, held, (o1, o2))


def solution(mesh):
    return jax.shard_map(
        per_device,
        mesh=mesh,
        in_specs=(
            P("tile", "mem"),
            P("tile", None, "mem"),
            P("tile", None, "mem"),
            P("tile", None, "mem"),
            P("tile", None),
            P("tile"),
            P("tile", None),
            P("tile", None),
        ),
        out_specs=P("tile", "mem"),
        check_vma=False,
    )
```

```python
import functools
import math

import jax
import jax.numpy as jnp
from jax import lax
from jax.experimental import pallas as pl
from jax.experimental.pallas import tpu as pltpu
from jax.sharding import PartitionSpec as P

VMEM_LIMIT = 24 * 1024 * 1024
FIRST_LIMIT = 60 * 1024 * 1024
GROUPS = 4
DEPTH = 8
CORES = 2
SLOTS = 2
STEPS = 4
SMALL = pl.CostEstimate(flops=10**6, bytes_accessed=10**6, transcendentals=0)


def first_kernel(
    q_ref, obs_ref, inv_ref, innov_ref, precision_ref, count_ref,
    gain_ref, innov_out_ref, m1_ref, m2_ref, m3_ref, rows_ref, live_ref,
):
    quarter, members = gain_ref.shape[1:]
    obs_rows, part = innov_ref.shape[1:]
    blocks = obs_ref.shape[0]
    q = q_ref[0]
    step = pl.program_id(0)
    position = lax.broadcasted_iota(jnp.int32, (obs_rows, part), 0)
    for k in range(blocks):
        rows_ref[...] = lax.dot_general(
            obs_ref[k], inv_ref[k], (((1,), (1,)), ((), ())), preferred_element_type=jnp.float32
        )
        block = step * blocks + k
        scale = jnp.broadcast_to(precision_ref[pl.ds(block, 1), :], (part, obs_rows)).T
        live_ref[...] = jnp.where(
            position < count_ref[block], scale * innov_ref[k].astype(jnp.float32), 0.0
        )
        own = pl.ds(pl.multiple_of(q * quarter, quarter), quarter)
        gain_ref[k] = rows_ref[own, :]
        innov_out_ref[k] = live_ref[own, :].astype(jnp.bfloat16)
        for d, ref in ((1, m1_ref), (2, m2_ref), (3, m3_ref)):
            rows = pl.ds(pl.multiple_of(lax.rem(q + d, GROUPS) * quarter, quarter), quarter)
            ref[k, :, :members] = rows_ref[rows, :].astype(jnp.bfloat16)
            ref[k, :, members:] = live_ref[rows, :].astype(jnp.bfloat16)


def first_parts(q, obs_anom, inverses, innovations, precision, obs_count):
    nblock, obs_rows, part = obs_anom.shape
    members = inverses.shape[1]
    quarter = obs_rows // GROUPS
    step = 8
    widths = [members, part] + [members + part] * 3
    types = [jnp.float32] + [jnp.bfloat16] * 4
    rows = pl.BlockSpec((step, obs_rows, part), lambda i, q: (i, 0, 0))
    return pl.pallas_call(
        first_kernel,
        grid_spec=pltpu.PrefetchScalarGridSpec(
            num_scalar_prefetch=1,
            grid=(nblock // step,),
            in_specs=[
                rows,
                pl.BlockSpec((step, members, part), lambda i, q: (i, 0, 0)),
                rows,
                pl.BlockSpec((nblock, obs_rows), lambda i, q: (0, 0)),
                pl.BlockSpec(memory_space=pltpu.SMEM),
            ],
            out_specs=[
                pl.BlockSpec((step, quarter, width), lambda i, q: (i, 0, 0)) for width in widths
            ],
            scratch_shapes=[
                pltpu.VMEM((obs_rows, members), jnp.float32),
                pltpu.VMEM((obs_rows, part), jnp.float32),
            ],
        ),
        out_shape=[
            jax.ShapeDtypeStruct((nblock, quarter, width), kind)
            for width, kind in zip(widths, types)
        ],
        compiler_params=pltpu.CompilerParams(vmem_limit_bytes=FIRST_LIMIT),
    )(q, obs_anom, inverses, innovations, precision, obs_count)


def merge_kernel(
    q_ref, early_ref, chosen_ref, taper_ref, gain_ref, innov_ref, r1_ref, r2_ref, r3_ref, low_ref, high_ref
):
    members = gain_ref.shape[2]
    part = innov_ref.shape[2]
    half = high_ref.shape[0]
    q = q_ref[0]
    gain = (
        gain_ref[...]
        + r1_ref[:, :, :members].astype(jnp.float32)
        + r2_ref[:, :, :members].astype(jnp.float32)
        + r3_ref[:, :, :members].astype(jnp.float32)
    ).astype(jnp.bfloat16)
    for out_ref, blocks in ((low_ref, slice(0, half)), (high_ref, slice(half, 2 * half))):
        out_ref[:half, :, :members] = gain[blocks]
        start = pl.multiple_of(members + q * part, part)
        out_ref[:half, :, pl.ds(start, part)] = innov_ref[blocks]
        for d, ref in ((1, r1_ref), (2, r2_ref), (3, r3_ref)):
            start = pl.multiple_of(members + lax.rem(q - d + GROUPS, GROUPS) * part, part)
            out_ref[:half, :, pl.ds(start, part)] = ref[blocks, :, members:]
    lanes = chosen_ref.shape[1]
    low_ref[half] = jnp.zeros(low_ref.shape[1:], low_ref.dtype)
    quarter = low_ref.shape[1]
    rest = jnp.broadcast_to(taper_ref[...], (quarter, lanes))
    low_ref[half, :, :lanes] = jnp.broadcast_to(chosen_ref[...], (quarter, lanes)).astype(jnp.bfloat16)
    for k in range(1, 4):
        term = rest.astype(jnp.bfloat16)
        rest = rest - term.astype(jnp.float32)
        low_ref[half, :, k * lanes : (k + 1) * lanes] = term


def merge(q, early, chosen, taper, parts):
    nblock, quarter, members = parts[0].shape
    half = nblock // 2
    vmem = pl.BlockSpec(memory_space=pltpu.VMEM)
    return pl.pallas_call(
        merge_kernel,
        in_specs=[pl.BlockSpec(memory_space=pltpu.SMEM)] * 2 + [vmem] * (2 + len(parts)),
        out_specs=[vmem] * 2,
        out_shape=[
            jax.ShapeDtypeStruct((half + 1, quarter, 2 * members), jnp.bfloat16),
            jax.ShapeDtypeStruct((half, quarter, 2 * members), jnp.bfloat16),
        ],
        compiler_params=pltpu.CompilerParams(vmem_limit_bytes=VMEM_LIMIT),
        cost_estimate=SMALL,
    )(q, early, chosen, taper, *parts)


def sums_kernel(same, token_ref, place_ref, *refs):
    lows, highs, refs = refs[:DEPTH], refs[DEPTH : 2 * DEPTH], refs[2 * DEPTH :]
    others, outs = (), ()
    if same:
        others, outs, refs = refs[:CORES], refs[CORES : CORES + GROUPS], refs[CORES + GROUPS :]
    else:
        outs, refs = refs[:CORES], refs[CORES:]
    pack = GROUPS // CORES
    all_ref, gain_ref, innov_ref, chosen_ref, taper_ref, chosen_smem, taper_smem, sems = refs
    half, quarter, width = highs[0].shape
    members = width // 2
    lanes = chosen_ref.shape[1]
    copies = []
    for k in range(DEPTH):
        copies.append(pltpu.make_async_copy(lows[k], all_ref.at[k, pl.ds(0, half + 1)], sems.at[2 * k]))
        copies.append(
            pltpu.make_async_copy(highs[k], all_ref.at[k, pl.ds(half + 1, half)], sems.at[2 * k + 1])
        )
    for copy in copies:
        copy.start()
    for k in range(DEPTH):
        copies[2 * k].wait()
        meta = all_ref[k, half, :, : 4 * lanes].astype(jnp.float32)[0:1]
        block = meta[:, :lanes].astype(jnp.int32)
        chosen_ref[pl.ds(k, 1), :] = block + jnp.where(block < half, 0, 1)
        taper_ref[pl.ds(k, 1), :] = (
            meta[:, lanes : 2 * lanes] + meta[:, 2 * lanes : 3 * lanes] + meta[:, 3 * lanes :]
        )
    tables = [
        pltpu.make_async_copy(chosen_ref, chosen_smem, sems.at[2 * DEPTH]),
        pltpu.make_async_copy(taper_ref, taper_smem, sems.at[2 * DEPTH + 1]),
    ]
    for copy in tables:
        copy.start()
    for k in range(DEPTH):
        copies[2 * k + 1].wait()
    for copy in tables:
        copy.wait()
    core = place_ref[2] if same else 1 - place_ref[2]
    for away in range(GROUPS):
        column = lax.rem(place_ref[0] + away, GROUPS)
        tile = (column * DEPTH + place_ref[1]) * CORES + core
        for k in range(DEPTH):
            for r in range(SLOTS):
                entry = r * (lanes // SLOTS) + tile
                block = chosen_smem[k, entry]
                rows = pl.ds((k * SLOTS + r) * quarter, quarter)
                gain = all_ref[k, block, :, :members].astype(jnp.float32)
                gain_ref[away, rows, :] = (taper_smem[k, entry] * gain).astype(jnp.bfloat16)
                innov_ref[away, rows, :] = all_ref[k, block, :, members:]
        total = lax.dot_general(
            gain_ref[away],
            innov_ref[away],
            (((0,), (0,)), ((), ())),
            preferred_element_type=jnp.float32,
        )
        if same:
            total = total + others[away // pack][away % pack].astype(jnp.float32)
            outs[away][...] = total.astype(outs[away].dtype)
        else:
            outs[away // pack][away % pack] = total.astype(jnp.bfloat16)


def sums(same, token, place, lows, highs, others=()):
    half, quarter, width = highs[0].shape
    members = width // 2
    lanes = 128
    square = (members, members)
    if same:
        kinds = [jnp.float32] + [jnp.bfloat16] * (GROUPS - 1)
        out_shape = [jax.ShapeDtypeStruct(square, kind) for kind in kinds]
    else:
        shape = (GROUPS // CORES,) + square
        out_shape = [jax.ShapeDtypeStruct(shape, jnp.bfloat16)] * CORES
    taken = (GROUPS, DEPTH * SLOTS * quarter, members)
    return pl.pallas_call(
        functools.partial(sums_kernel, same),
        in_specs=[pl.BlockSpec(memory_space=pltpu.SMEM)] * 2
        + [pl.BlockSpec(memory_space=pl.ANY)] * (2 * DEPTH)
        + [pl.BlockSpec(memory_space=pltpu.VMEM)] * len(others),
        out_specs=[pl.BlockSpec(memory_space=pltpu.VMEM)] * len(out_shape),
        out_shape=out_shape,
        scratch_shapes=[
            pltpu.VMEM((DEPTH, 2 * half + 1, quarter, width), jnp.bfloat16),
            pltpu.VMEM(taken, jnp.bfloat16),
            pltpu.VMEM(taken, jnp.bfloat16),
            pltpu.VMEM((DEPTH, lanes), jnp.int32),
            pltpu.VMEM((DEPTH, lanes), jnp.float32),
            pltpu.SMEM((DEPTH, lanes), jnp.int32),
            pltpu.SMEM((DEPTH, lanes), jnp.float32),
            pltpu.SemaphoreType.DMA((2 * DEPTH + 2,)),
        ],
        compiler_params=pltpu.CompilerParams(vmem_limit_bytes=VMEM_LIMIT),
        cost_estimate=SMALL,
    )(token, place, *lows, *highs, *others)


def arrived_kernel(*refs):
    refs[-1][0] = 0


def arrived(*arrays):
    return pl.pallas_call(
        arrived_kernel,
        in_specs=[pl.BlockSpec(memory_space=pl.ANY)] * len(arrays),
        out_specs=pl.BlockSpec(memory_space=pltpu.SMEM),
        out_shape=jax.ShapeDtypeStruct((1,), jnp.int32),
        cost_estimate=pl.CostEstimate(flops=10**12, bytes_accessed=10**9, transcendentals=0),
    )(*arrays)


def transform_kernel(q_ref, token_ref, r0_ref, r1_ref, r2_ref, r3_ref, own_ref, s1_ref, s2_ref, s3_ref):
    q = q_ref[0]
    members, part = own_ref.shape
    for d, out_ref in enumerate((own_ref, s1_ref, s2_ref, s3_ref)):
        columns = pl.ds(pl.multiple_of(lax.rem(q + d, GROUPS) * part, part), part)
        total = (
            r0_ref[:, columns]
            + r1_ref[:, columns].astype(jnp.float32)
            + r2_ref[:, columns].astype(jnp.float32)
            + r3_ref[:, columns].astype(jnp.float32)
        )
        mean = jnp.sum(total, axis=0, keepdims=True) / members
        out_ref[...] = ((total - mean) * (1.0 / math.sqrt(members - 1))).astype(out_ref.dtype)


def transform_parts(q, token, sums_here):
    members = sums_here[0].shape[0]
    part = members // GROUPS
    return pl.pallas_call(
        transform_kernel,
        in_specs=[pl.BlockSpec(memory_space=pltpu.SMEM)] * 2
        + [pl.BlockSpec(memory_space=pltpu.VMEM)] * GROUPS,
        out_specs=[pl.BlockSpec(memory_space=pltpu.VMEM)] * GROUPS,
        out_shape=[jax.ShapeDtypeStruct((members, part), jnp.float32)]
        + [jax.ShapeDtypeStruct((members, part), jnp.bfloat16)] * 3,
        compiler_params=pltpu.CompilerParams(vmem_limit_bytes=VMEM_LIMIT),
        cost_estimate=pl.CostEstimate(flops=5*10**9, bytes_accessed=10**6, transcendentals=0),
    )(q, token, *sums_here)


def hold_kernel(own_ref, a1_ref, a2_ref, b1_ref, b2_ref, out_ref, sems):
    half = a1_ref.shape[0]
    copies = [pltpu.make_async_copy(own_ref, out_ref.at[0], sems.at[0])]
    for k, (low, high) in enumerate(((a1_ref, a2_ref), (b1_ref, b2_ref))):
        copies.append(
            pltpu.make_async_copy(low, out_ref.at[k + 1, pl.ds(0, half)], sems.at[2 * k + 1])
        )
        copies.append(
            pltpu.make_async_copy(high, out_ref.at[k + 1, pl.ds(half, half)], sems.at[2 * k + 2])
        )
    for copy in copies:
        copy.start()
    for copy in copies:
        copy.wait()


def hold(own, others):
    rows, part = own.shape
    return pl.pallas_call(
        hold_kernel,
        in_specs=[pl.BlockSpec(memory_space=pl.ANY)] * (1 + len(others)),
        out_specs=pl.BlockSpec(memory_space=pltpu.VMEM),
        out_shape=jax.ShapeDtypeStruct((GROUPS - 1, rows, part), jnp.bfloat16),
        scratch_shapes=[pltpu.SemaphoreType.DMA((5,))],
        compiler_params=pltpu.CompilerParams(vmem_limit_bytes=16 * 1024 * 1024),
        cost_estimate=SMALL,
    )(own, *others)


def update_kernel(
    order_ref, t0_ref, t1_ref, t2_ref, t3_ref, held_ref, o1_ref, o2_ref,
    out_ref, raw_ref, weights_ref, far_ref, result_ref, in_sems, out_sems,
):
    part = held_ref.shape[2]
    step = result_ref.shape[1]
    half = STEPS // 2
    loads = []
    for i in range(STEPS):
        ref = o1_ref if i < half else o2_ref
        loads.append(
            pltpu.make_async_copy(ref.at[pl.ds((i % half) * step, step)], far_ref.at[i], in_sems.at[i])
        )
        loads[-1].start()
    total = (
        t0_ref[...]
        + t1_ref[...].astype(jnp.float32)
        + t2_ref[...].astype(jnp.float32)
        + t3_ref[...].astype(jnp.float32)
    ).astype(jnp.bfloat16)
    raw_ref[...] = total.reshape(raw_ref.shape)
    for k in range(GROUPS):
        weights_ref[pl.ds(k * part, part), :] = raw_ref[order_ref[k]]
    stores = []
    for i in range(STEPS):
        loads[i].wait()
        rows = pl.ds(i * step, step)
        near = [held_ref[k, rows, :] for k in range(GROUPS - 1)]
        states = jnp.concatenate(near + [far_ref[i]], axis=1)
        increment = jnp.dot(states, weights_ref[...], preferred_element_type=jnp.float32)
        result_ref[i] = (near[0].astype(jnp.float32) + increment).astype(result_ref.dtype)
        stores.append(pltpu.make_async_copy(result_ref.at[i], out_ref.at[rows], out_sems.at[i]))
        stores[-1].start()
    for store in stores:
        store.wait()


def update(order, pieces, held, others):
    rows, part = held.shape[1:]
    members = pieces[0].shape[0]
    step = rows // STEPS
    return pl.pallas_call(
        update_kernel,
        in_specs=[pl.BlockSpec(memory_space=pltpu.SMEM)]
        + [pl.BlockSpec(memory_space=pltpu.VMEM)] * (GROUPS + 1)
        + [pl.BlockSpec(memory_space=pl.ANY)] * len(others),
        out_specs=pl.BlockSpec(memory_space=pl.ANY),
        out_shape=jax.ShapeDtypeStruct((rows, part), jnp.bfloat16),
        scratch_shapes=[
            pltpu.VMEM((GROUPS, part, part), jnp.bfloat16),
            pltpu.VMEM((members, part), jnp.bfloat16),
            pltpu.VMEM((STEPS, step, part), jnp.bfloat16),
            pltpu.VMEM((STEPS, step, part), jnp.bfloat16),
            pltpu.SemaphoreType.DMA((STEPS,)),
            pltpu.SemaphoreType.DMA((STEPS,)),
        ],
        compiler_params=pltpu.CompilerParams(vmem_limit_bytes=VMEM_LIMIT),
    )(order, *pieces, held, *others)


def shift(x, d):
    return lax.ppermute(x, "mem", [(i, (i + d) % GROUPS) for i in range(GROUPS)])


def swap_a(x):
    return lax.ppermute(x, "mem", [(0, 1), (1, 0), (2, 3), (3, 2)])


def swap_b(x):
    return lax.ppermute(x, "mem", [(0, 3), (3, 0), (1, 2), (2, 1)])


def move(x, columns, away=(0, 0, 0)):
    pairs = []
    for c in range(columns):
        for z in range(DEPTH):
            for k in range(CORES):
                target = (c + away[0]) % columns, (z + away[1]) % DEPTH, (k + away[2]) % CORES
                pairs.append(
                    ((c * DEPTH + z) * CORES + k, (target[0] * DEPTH + target[1]) * CORES + target[2])
                )
    return lax.ppermute(x, "tile", pairs)


def per_device(
    ensemble, obs_anom, inverses, innovations, precision, obs_count, loc_tiles, taper_weight
):
    columns = lax.axis_size("tile") // (DEPTH * CORES)
    nblock = obs_anom.shape[0]
    rows = ensemble.shape[0]
    loc_count = loc_tiles.shape[1]
    pairs = nblock * loc_count
    q = lax.axis_index("mem").astype(jnp.int32)
    q1 = q.reshape(1)
    order = jnp.stack([q, q ^ 1, 3 - q, q ^ 2])
    tile = lax.axis_index("tile").astype(jnp.int32)
    place = jnp.stack([tile // (DEPTH * CORES), (tile // CORES) & (DEPTH - 1), tile & (CORES - 1)])

    gain, innov, m1, m2, m3 = first_parts(
        q1, obs_anom, inverses, innovations, precision, obs_count
    )
    m1, m2, m3 = shift(m1, 1), shift(m2, 2), shift(m3, 3)

    tiles = columns * DEPTH * CORES
    loc = loc_tiles.reshape(pairs, 1)
    hits = (loc == lax.broadcasted_iota(jnp.int32, (pairs, tiles), 1)).astype(jnp.float32)
    same_tile = (loc == loc_tiles.reshape(1, pairs)).astype(jnp.float32)
    pair_at = lax.broadcasted_iota(jnp.int32, (pairs, 1), 0)
    earlier = (lax.broadcasted_iota(jnp.int32, (pairs, pairs), 1) < pair_at).astype(jnp.float32)
    rank = jnp.sum(same_tile * earlier, axis=1, keepdims=True)
    ranked = jnp.concatenate([hits * (rank == r).astype(jnp.float32) for r in range(SLOTS)], axis=1)
    block_of = (pair_at // loc_count).astype(jnp.float32)
    chosen = jnp.sum(ranked * block_of, axis=0, keepdims=True)
    tapers = jnp.sum(ranked * taper_weight.reshape(pairs, 1), axis=0, keepdims=True)

    half = rows // 2
    early = arrived(m1, m3)
    m1, low, high = lax.optimization_barrier((m1, ensemble[:half], ensemble[half:]))
    a2, b1 = swap_a(high), swap_b(low)
    a1, b2 = swap_a(low), swap_b(high)

    up, down = (0, 1, 0), (0, -1, 0)
    own_blocks = tuple(merge(q1, early, chosen, tapers, (gain, innov, m1, m2, m3)))
    ups, downs = [own_blocks], [own_blocks]
    for _ in range(3):
        ups.append(tuple(move(x, columns, up) for x in ups[-1]))
        downs.append(tuple(move(x, columns, down) for x in downs[-1]))
    token = arrived(a2, b1)
    token, far = lax.optimization_barrier((token, (ups[-1][0], downs[-1][1])))
    far = (move(far[0], columns, up), move(far[1], columns, down))
    held = ups + downs[1:] + [far]
    lows, highs = [h[0] for h in held], [h[1] for h in held]
    others = sums(0, token, place, lows, highs)
    others = [move(x, columns, (0, 0, 1)) for x in others]
    here, e1, e2, e3 = sums(1, token, place, lows, highs, others)
    here, a1 = lax.optimization_barrier((here, a1))
    e2, b2 = lax.optimization_barrier((e2, b2))
    o1, o2 = swap_b(a1), swap_a(b2)
    e1, e2, e3 = move(e1, columns, (1, 0, 0)), move(e2, columns, (2, 0, 0)), move(e3, columns, (3, 0, 0))
    t0, t1, t2, t3 = transform_parts(q1, token, (here, e1, e2, e3))
    pieces = [t0, shift(t1, 1), shift(t2, 2), shift(t3, 3)]
    held = hold(ensemble, (a1, a2, b1, b2))
    return update(order, pieces, held, (o1, o2))


def solution(mesh):
    return jax.shard_map(
        per_device,
        mesh=mesh,
        in_specs=(
            P("tile", "mem"),
            P("tile", None, "mem"),
            P("tile", None, "mem"),
            P("tile", None, "mem"),
            P("tile", None),
            P("tile"),
            P("tile", None),
            P("tile", None),
        ),
        out_specs=P("tile", "mem"),
        check_vma=False,
    )
```
